512 devices in a mesh: dom: 64 (over z, x), elem: 8 (over y, core).
Axes of the slice: x: 4, y: 4, z: 16, core: 2. Of those that a mesh axis runs over, the one named last changes fastest.
Arguments:
- adjoint: float32 [4, 125, 131072], P(None, None, ('dom', 'elem')), may hold values from -6 to 6
- adjoint_reg: float32 [4, 125, 131072], P(None, None, ('dom', 'elem')), may hold values from -4 to 4
- metric: float32 [3, 131072], P(None, ('dom', 'elem')), may hold values from 1 to 4
- face_link: int32 [6, 131072], P(None, ('dom', 'elem')), may hold values from -1 to 2815, as said below
- orient: int32 [6, 131072], P(None, ('dom', 'elem')), may hold values from 0 to 7
- intra_send: int32 [65536], P(('dom', 'elem')), may hold values from 0 to 1535
- part_send: int32 [4, 32768], P(None, ('dom', 'elem')), may hold values from 0 to 1535
- wall_face: int32 [65536], P(('dom', 'elem')), may hold values from -1 to 1535, as said below
- wall_patch: int32 [65536], P(('dom', 'elem')), may hold values from 0 to 4095
- pole_count: int32 [4096], replicated, may hold values from 1 to 6
- amplitude: float32 [4096, 6], replicated, may hold values from -4 to 4
- pole_decay: float32 [4096, 6], replicated, may hold values from 0.5 to 10
- wall_aux: float32 [6, 25, 65536], P(None, None, ('dom', 'elem')), may hold values from -6 to 6
- wall_aux_reg: float32 [6, 25, 65536], P(None, None, ('dom', 'elem')), may hold values from -4 to 4
- forward_aux: bfloat16 [2, 6, 25, 65536], P(None, None, None, ('dom', 'elem')), may hold values from -6 to 6
Outputs:
- adjoint_out: float32 [4, 125, 131072], P(None, None, ('dom', 'elem'))
- adjoint_reg_out: float32 [4, 125, 131072], P(None, None, ('dom', 'elem'))
- wall_aux_out: float32 [6, 25, 65536], P(None, None, ('dom', 'elem'))
- wall_aux_reg_out: float32 [6, 25, 65536], P(None, None, ('dom', 'elem'))
- patch_grad: float32 [4096, 6], P(('dom', 'elem'))
The draws below stay inside these ranges and needn't reach their ends.
Inputs may be any that keep to these rules, and one draw needn't show every extreme that they name: `face_link`: -1 marks a wall face; on each device the faces marked -1 are exactly those listed in its block of wall_face. `wall_face`: each device's block lists distinct faces first and -1 in the remaining slots; at most 128 wall faces a device, and some device has all 128 slots filled.
All inputs are finite; a program needn't handle non-finite values.
Results may differ from the reference program's by a relative error of at most 0.00035.
Values sent between devices are 32-bit elements; how exact they have to be, the bound alone decides.
A program may use at most 64 MiB of HBM per device.

```python
import math
import jax
import jax.numpy as jnp
import numpy as np
from jax import lax

E_DEV = 256
POLES = 6
PATCHES = 4096
SECTIONS = 2
ICAP = 128
DCAP = 64
WCAP = 128
ELEMS = 131072
N_DOM = 64
N_ELEM = 8


def wall_layout(key):
    device_count = N_DOM * N_ELEM
    face_count = 6 * E_DEV
    key_counts, key_full, key_order = jax.random.split(key, 3)
    counts = jax.random.randint(key_counts, (device_count,), WCAP // 8, WCAP // 2 + 1)
    fullest = jax.random.randint(key_full, (), 0, device_count)
    counts = jnp.where(jnp.arange(device_count) == fullest, WCAP, counts)
    orders = jax.vmap(lambda subkey: jax.random.permutation(subkey, face_count))(jax.random.split(key_order, device_count))
    return (counts.astype(jnp.int32), orders.astype(jnp.int32))


def draw_wall_face(key, part):
    counts, orders = wall_layout(key)
    slot_index = jnp.arange(WCAP, dtype=jnp.int32)
    table = jnp.where(slot_index[None, :] < counts[:, None], orders[:, :WCAP], -1)
    return table.reshape(-1).astype(jnp.int32)


def draw_face_link(key, part):
    counts, orders = wall_layout(key)
    key = jax.random.fold_in(key, 5)
    device_count = N_DOM * N_ELEM
    face_count = 6 * E_DEV
    key_kind, key_local, key_intra, key_part = jax.random.split(key, 4)
    grid_shape = (device_count, face_count)
    kind_pick = jax.random.randint(key_kind, grid_shape, 0, 8)
    local_pick = jax.random.randint(key_local, grid_shape, 0, face_count)
    intra_pick = face_count + jax.random.randint(key_intra, grid_shape, 0, N_ELEM * ICAP)
    part_pick = face_count + N_ELEM * ICAP + jax.random.randint(key_part, grid_shape, 0, 4 * DCAP)
    link_table = jnp.where(kind_pick < 4, local_pick, jnp.where(kind_pick < 6, intra_pick, part_pick))
    position = jnp.argsort(orders, axis=1).astype(jnp.int32)
    link_table = jnp.where(position < counts[:, None], -1, link_table)
    link_table = jnp.where(position == face_count - 1, face_count + N_ELEM * ICAP + 4 * DCAP - 1, link_table)
    link_table = link_table.reshape(device_count, 6, E_DEV).transpose(1, 0, 2).reshape(6, device_count * E_DEV)
    return link_table.astype(jnp.int32)


def plant(entries, stream_key, least, top_value):
    longest = entries.shape.index(max(entries.shape))
    spots = []
    for shift in (0, 1):
        where = [jax.random.randint(jax.random.fold_in(stream_key, axis), (), 0, length) for axis, length in enumerate(entries.shape)]
        where[longest] = (where[longest] + shift) % entries.shape[longest]
        spots.append(tuple(where))
    return entries.at[spots[0]].set(least).at[spots[1]].set(top_value)


def block_scale(own_key, extent, cuts, least, high):
    def one(dim, shards_of):
        heights = jax.random.uniform(jax.random.fold_in(jax.random.fold_in(own_key, 6), dim), (shards_of,), jnp.float32, least / len(cuts), high / len(cuts))
        return jnp.repeat(jnp.exp(heights), extent[dim] // shards_of).reshape((-1,) + (1,) * (len(extent) - dim - 1))

    level = one(*cuts[0])
    for cut in cuts[1:]:
        level = level * one(*cut)
    return level


def normal_values(rng, dims, spread, limit, cuts=(), kind=jnp.bfloat16):
    drawn = spread * jax.random.normal(rng, dims, jnp.float32)
    if cuts:
        drawn = drawn * block_scale(rng, dims, cuts, -0.22, 0.18)
    return jnp.clip(drawn, -limit, limit).astype(kind)


def setup_inputs(seed: int = 0) -> dict:
    splits = jax.random.split(jax.random.key(seed), 16)
    adjoint = normal_values(splits[0], (4, 125, ELEMS), 1.0, 6.0, ((2, 512),), jnp.float32)
    adjoint_reg = normal_values(splits[1], (4, 125, ELEMS), 0.5, 4.0, ((2, 512),), jnp.float32)
    metric = jnp.clip(jnp.exp(math.log(4.0) - 1.3862944 * jax.random.uniform(splits[2], (3, ELEMS), jnp.float32) ** block_scale(splits[2], (3, ELEMS), ((1, 512),), -0.2, 0.2)), 1.0, 4.0)
    face_link = draw_face_link(jax.random.fold_in(splits[15], 71), 0)
    orient = plant(jax.random.randint(splits[4], (6, ELEMS), 0, 8), jax.random.fold_in(splits[4], 1), 0, 7).astype(jnp.int32)
    intra_send = plant(jax.random.randint(splits[5], (ICAP * N_DOM * N_ELEM,), 0, 6 * E_DEV), jax.random.fold_in(splits[5], 1), 0, (6 * E_DEV) - 1).astype(jnp.int32)
    part_send = plant(jax.random.randint(splits[6], (4, DCAP * N_DOM * N_ELEM), 0, 6 * E_DEV), jax.random.fold_in(splits[6], 1), 0, (6 * E_DEV) - 1).astype(jnp.int32)
    wall_face = draw_wall_face(jax.random.fold_in(splits[15], 71), 0)
    wall_patch = plant(jax.random.randint(splits[8], (WCAP * N_DOM * N_ELEM,), 0, PATCHES), jax.random.fold_in(splits[8], 1), 0, PATCHES - 1).astype(jnp.int32)
    pole_count = plant(jax.random.randint(splits[9], (PATCHES,), 1, POLES + 1), jax.random.fold_in(splits[9], 1), 1, POLES).astype(jnp.int32)
    amplitude = normal_values(splits[10], (PATCHES, POLES), 1.0, 4.0, (), jnp.float32)
    pole_decay = jnp.clip(jnp.exp(jax.random.uniform(splits[11], (PATCHES, POLES), jnp.float32, math.log(0.5), math.log(10.0))), 0.5, 10.0)
    wall_aux = normal_values(splits[12], (POLES, 25, WCAP * N_DOM * N_ELEM), 1.0, 6.0, ((2, 512),), jnp.float32)
    wall_aux_reg = normal_values(splits[13], (POLES, 25, WCAP * N_DOM * N_ELEM), 0.5, 4.0, ((2, 512),), jnp.float32)
    forward_aux = normal_values(splits[14], (SECTIONS, POLES, 25, WCAP * N_DOM * N_ELEM), 1.0, 6.0, ((3, 512),))
    return dict(adjoint=adjoint, adjoint_reg=adjoint_reg, metric=metric, face_link=face_link, orient=orient, intra_send=intra_send, part_send=part_send, wall_face=wall_face, wall_patch=wall_patch, pole_count=pole_count, amplitude=amplitude, pole_decay=pole_decay, wall_aux=wall_aux, wall_aux_reg=wall_aux_reg, forward_aux=forward_aux)


DT_STEP = 0.1
SECTION_A = (-1.514183444257, -1.697784692471)
SECTION_B = (0.1530572479681, 0.6994504559488)
OFFSETS = (-2, -1, 1, 2)
PRECISE = lax.Precision.HIGHEST

def lobatto_tables():
    node_points = np.array([-1.0, -np.sqrt(3.0 / 7.0), 0.0, np.sqrt(3.0 / 7.0), 1.0])
    quad_line = np.array([0.1, 49.0 / 90.0, 32.0 / 45.0, 49.0 / 90.0, 0.1])
    bary_weight = np.array([1.0 / np.prod([node_points[j] - node_points[k] for k in range(5) if k != j]) for j in range(5)])
    line_deriv = np.zeros((5, 5))
    for i in range(5):
        for j in range(5):
            if i != j:
                line_deriv[i, j] = bary_weight[j] / bary_weight[i] / (node_points[i] - node_points[j])
        line_deriv[i, i] = -np.sum(line_deriv[i])
    return (line_deriv, quad_line)

def dense_tables():
    line_deriv, quad_line = lobatto_tables()
    identity = np.eye(5)
    along_axes = [np.kron(np.kron(line_deriv, identity), identity), np.kron(np.kron(identity, line_deriv), identity), np.kron(np.kron(identity, identity), line_deriv)]
    return (jnp.asarray(np.concatenate(along_axes, 0), jnp.float32), jnp.asarray(np.concatenate(along_axes, 1), jnp.float32))

def face_traces(node_grid):
    face_list = [node_grid[:, 0], node_grid[:, 4], node_grid[:, :, 0], node_grid[:, :, 4], node_grid[:, :, :, 0], node_grid[:, :, :, 4]]
    return jnp.stack(face_list, axis=3)

def orient_faces(gathered, orient_flat):
    result = gathered
    for symmetry in range(1, 8):
        variant = gathered
        if symmetry & 4:
            variant = jnp.swapaxes(variant, 1, 2)
        if symmetry & 1:
            variant = variant[:, ::-1]
        if symmetry & 2:
            variant = variant[:, :, ::-1]
        result = jnp.where(orient_flat == symmetry, variant, result)
    return result

def volume_dense(adjoint_now, metric_dev):
    stack_table, concat_table = dense_tables()
    elements = adjoint_now.shape[-1]
    grads = jnp.dot(stack_table, adjoint_now[0], precision=PRECISE, preferred_element_type=jnp.float32)
    grads = grads.reshape(3, 125, elements) * metric_dev[:, None, :]
    scaled = (adjoint_now[1:4] * metric_dev[:, None, :]).reshape(375, elements)
    diverge = jnp.dot(concat_table, scaled, precision=PRECISE, preferred_element_type=jnp.float32)
    return jnp.concatenate([-diverge[None], -grads], axis=0)

def lift_faces(residual, face_flux, metric_dev):
    elements = residual.shape[-1]
    grid_residual = residual.reshape(4, 5, 5, 5, elements)
    for face_id in range(6):
        axis_id = face_id // 2
        edge_node = 0 if face_id % 2 == 0 else 4
        normal_sign = -1.0 if face_id % 2 == 0 else 1.0
        lifted = 10.0 * metric_dev[axis_id] * face_flux[:, :, face_id]
        position = (slice(None),) * axis_id + (edge_node,)
        grid_residual = grid_residual.at[(0,) + position].add(lifted)
        grid_residual = grid_residual.at[(1 + axis_id,) + position].add(-normal_sign * lifted)
    return grid_residual.reshape(4, 125, elements)

def section_update(adjoint_now, register, trace_grid, trace_pool, metric_dev, link_dev, orient_dev, wall_dev, patch_dev, pole_count, amplitude, pole_decay, aux_state, aux_reg, forward_dev, section_id, volume):
    elements = adjoint_now.shape[-1]
    face_count = 6 * elements
    coef_a = SECTION_A[section_id]
    coef_b = SECTION_B[section_id]
    link_flat = link_dev.reshape(-1)
    is_wall = link_flat < 0
    near_trace = jnp.take(trace_pool, jnp.where(is_wall, 0, link_flat), axis=1).reshape(4, 5, 5, face_count)
    near_trace = orient_faces(near_trace, orient_dev.reshape(-1))
    own_trace = trace_grid.reshape(4, 5, 5, face_count)
    face_of = jnp.arange(face_count, dtype=jnp.int32) // elements
    axis_of = face_of // 2
    sign_of = jnp.where(face_of % 2 == 0, -1.0, 1.0).astype(jnp.float32)

    def normal_part(face_grid):
        return sign_of * jnp.where(axis_of == 0, face_grid[1], jnp.where(axis_of == 1, face_grid[2], face_grid[3]))
    un_own = normal_part(own_trace).reshape(25, face_count)
    un_near = normal_part(near_trace).reshape(25, face_count)
    live_slot = wall_dev >= 0
    un_slot = jnp.take(un_own, jnp.where(live_slot, wall_dev, 0), axis=1) * live_slot.astype(jnp.float32)
    pole_total = amplitude.shape[1]
    active = ((jnp.arange(pole_total, dtype=jnp.int32)[:, None] < jnp.take(pole_count, patch_dev)[None, :]) & live_slot[None, :]).astype(jnp.float32)
    amp_slot = jnp.take(amplitude, patch_dev, axis=0).T
    decay_slot = jnp.take(pole_decay, patch_dev, axis=0).T
    wall_value = lax.optimization_barrier(jnp.sum((active * amp_slot)[:, None, :] * aux_state, axis=0))
    wall_face_value = jnp.zeros((25, face_count), jnp.float32).at[:, jnp.where(live_slot, wall_dev, face_count)].set(wall_value, mode='drop')
    jump_p = jnp.where(is_wall, 0.0, (near_trace[0] - own_trace[0]).reshape(25, face_count))
    jump_un = jnp.where(is_wall, 2.0 * wall_face_value - 2.0 * un_own, un_near - un_own)
    face_flux = (0.5 * (jump_p - jump_un)).reshape(5, 5, 6, elements)
    residual = lift_faces(volume(adjoint_now, metric_dev), face_flux, metric_dev)
    register = coef_a * register + DT_STEP * residual
    adjoint_now = adjoint_now + coef_b * register
    aux_rate = active[:, None, :] * (un_slot[None] - decay_slot[:, None, :] * aux_state)
    aux_reg = coef_a * aux_reg + DT_STEP * aux_rate
    aux_state = aux_state + coef_b * aux_reg
    line_deriv, quad_line = lobatto_tables()
    quad_weight = jnp.asarray(np.outer(quad_line, quad_line).reshape(25), jnp.float32)
    grad_term = coef_b * DT_STEP * active * lax.optimization_barrier(jnp.sum(quad_weight[None, :, None] * un_slot[None] * forward_dev, axis=1))
    partial_value = jax.ops.segment_sum(grad_term.T, patch_dev, num_segments=amplitude.shape[0])
    return (adjoint_now, register, aux_state, aux_reg, partial_value)

def device_block(array, device_id, width):
    return lax.dynamic_slice_in_dim(array, device_id * width, width, array.ndim - 1)

def global_section(state_list, metric, face_link, orient, intra_send, part_send, wall_face, wall_patch, pole_count, amplitude, pole_decay, forward_section, section_id):
    adjoint, adjoint_reg, wall_aux, wall_aux_reg = state_list
    device_ids = jnp.arange(N_DOM * N_ELEM, dtype=jnp.int32)

    def send_side(device_id):
        trace_grid = face_traces(device_block(adjoint, device_id, E_DEV).reshape(4, 5, 5, 5, E_DEV))
        flat_traces = trace_grid.reshape(100, 6 * E_DEV)
        return (jnp.take(flat_traces, device_block(intra_send, device_id, ICAP), axis=1), jnp.take(flat_traces, device_block(part_send, device_id, DCAP), axis=1))
    intra_all, outward_all = lax.map(send_side, device_ids)

    def receive_side(device_id):
        dom_id = device_id // N_ELEM
        elem_id = device_id % N_ELEM
        adjoint_now = device_block(adjoint, device_id, E_DEV)
        trace_grid = face_traces(adjoint_now.reshape(4, 5, 5, 5, E_DEV))
        part_rows = lax.dynamic_slice_in_dim(intra_all, dom_id * N_ELEM, N_ELEM, 0)
        pieces = [trace_grid.reshape(100, 6 * E_DEV), jnp.moveaxis(part_rows, 0, 1).reshape(100, N_ELEM * ICAP)]
        for slot_id, offset in enumerate(OFFSETS):
            source = (dom_id - offset) % N_DOM * N_ELEM + elem_id
            pieces.append(outward_all[source][:, slot_id])
        trace_pool = jnp.concatenate(pieces, axis=1)
        return section_update(adjoint_now, device_block(adjoint_reg, device_id, E_DEV), trace_grid, trace_pool, device_block(metric, device_id, E_DEV), device_block(face_link, device_id, E_DEV), device_block(orient, device_id, E_DEV), device_block(wall_face, device_id, WCAP), device_block(wall_patch, device_id, WCAP), pole_count, amplitude, pole_decay, device_block(wall_aux, device_id, WCAP), device_block(wall_aux_reg, device_id, WCAP), device_block(forward_section, device_id, WCAP), section_id, volume_dense)
    new_adjoint, new_reg, new_aux, new_aux_reg, partial_value = lax.map(receive_side, device_ids)
    new_adjoint = jnp.transpose(new_adjoint, (1, 2, 0, 3)).reshape(4, 125, ELEMS)
    new_reg = jnp.transpose(new_reg, (1, 2, 0, 3)).reshape(4, 125, ELEMS)
    new_aux = jnp.transpose(new_aux, (1, 2, 0, 3)).reshape(POLES, 25, WCAP * N_DOM * N_ELEM)
    new_aux_reg = jnp.transpose(new_aux_reg, (1, 2, 0, 3)).reshape(POLES, 25, WCAP * N_DOM * N_ELEM)
    return ((new_adjoint, new_reg, new_aux, new_aux_reg), lax.optimization_barrier(jnp.sum(partial_value, axis=0)))

def reference(adjoint, adjoint_reg, metric, face_link, orient, intra_send, part_send, wall_face, wall_patch, pole_count, amplitude, pole_decay, wall_aux, wall_aux_reg, forward_aux):
    state_list = (adjoint, adjoint_reg, wall_aux, wall_aux_reg)
    grad_total = jnp.zeros((PATCHES, POLES), jnp.float32)
    for section_id in range(SECTIONS):
        state_list, partial_value = global_section(state_list, metric, face_link, orient, intra_send, part_send, wall_face, wall_patch, pole_count, amplitude, pole_decay, forward_aux[section_id].astype(jnp.float32), section_id)
        grad_total = grad_total + partial_value
    return (state_list[0], state_list[1], state_list[2], state_list[3], grad_total)
```

```python
import functools

import jax
import jax.numpy as jnp
import numpy as np
from jax import lax
from jax.experimental import pallas as pl
from jax.experimental.pallas import tpu as pltpu
from jax.sharding import PartitionSpec as P

DT_STEP = 0.1
SECTION_A = (-1.514183444257, -1.697784692471)
SECTION_B = (0.1530572479681, 0.6994504559488)
OFFSETS = (-2, -1, 1, 2)
ELEM_ORDER = (1, 7, 2, 6, 3, 5, 4)
N_ELEM, N_DOM, NX, NZ = 8, 64, 4, 16
OWN, FAR = 12, 20
CHUNKS = 24
ROWS = 104
F32 = jnp.float32
I32 = jnp.int32
FACE_NODE = ((0, 5, 1), (100, 5, 1), (0, 25, 1), (20, 25, 1), (0, 25, 5), (4, 25, 5))
MESH = pl.DeviceIdType.MESH


def lobatto_tables():
    node_points = np.array([-1.0, -np.sqrt(3.0 / 7.0), 0.0, np.sqrt(3.0 / 7.0), 1.0])
    quad_line = np.array([0.1, 49.0 / 90.0, 32.0 / 45.0, 49.0 / 90.0, 0.1])
    bary_weight = np.array(
        [
            1.0 / np.prod([node_points[j] - node_points[k] for k in range(5) if k != j])
            for j in range(5)
        ]
    )
    line_deriv = np.zeros((5, 5))
    for i in range(5):
        for j in range(5):
            if i != j:
                line_deriv[i, j] = (
                    bary_weight[j] / bary_weight[i] / (node_points[i] - node_points[j])
                )
        line_deriv[i, i] = -np.sum(line_deriv[i])
    return (line_deriv, quad_line)


def constant_tables():
    line_deriv, quad_line = lobatto_tables()
    eye = np.eye(5)
    stack = np.zeros((3, 128, 125), np.float32)
    stack[0, :125] = np.kron(np.kron(line_deriv, eye), eye)
    stack[1, :125] = np.kron(np.kron(eye, line_deriv), eye)
    stack[2, :125] = np.kron(np.kron(eye, eye), line_deriv)
    stack = stack.reshape(384, 125)
    high = stack.astype(jnp.bfloat16)
    low = (stack - high.astype(np.float32)).astype(jnp.bfloat16)
    weights = np.broadcast_to(np.outer(quad_line, quad_line).reshape(25, 1), (25, 128))
    grid = np.arange(25).reshape(5, 5)
    perm = np.zeros((8, 32, 64), np.float32)
    for symmetry in range(8):
        variant = grid
        if symmetry & 4:
            variant = variant.T
        if symmetry & 1:
            variant = variant[::-1]
        if symmetry & 2:
            variant = variant[:, ::-1]
        for row, source in enumerate(variant.reshape(-1)):
            perm[symmetry, row, source] = 1.0
            perm[symmetry, row, 32 + source] = 1.0
    return (
        jnp.asarray(high),
        jnp.asarray(low),
        jnp.asarray(perm.reshape(256, 64), jnp.bfloat16),
        jnp.asarray(weights, F32),
    )


def lane_take(values, index):
    return jnp.take_along_axis(values, index, axis=1, mode="promise_in_bounds")


def split(values):
    high = values.astype(jnp.bfloat16)
    return high, (values - high.astype(F32)).astype(jnp.bfloat16)


def rows_of(row, count):
    return jnp.broadcast_to(row, (count, 128))


def iota(shape, dim):
    return lax.broadcasted_iota(I32, shape, dim)


def kernel(
    adj_in, reg_in, metric, link, orient, isend, psend, wface, wpatch, pcount, amp, decay,
    aux_in, auxr_in, fwd, dhigh, dlow, perm, weights,
    adj_out, reg_out, aux_out, auxr_out, grad_out,
    A, R, S, pool, sendb, G, lift, wall, wslot, uslot, ampb, decb, T, Trecv, onehot, X, Xrecv, Z, Zrecv,
    load_sem, own_sem, si_sem, ri_sem, sp_sem, rp_sem, sg_sem, rg_sem, sx_sem, rx_sem, sz_sem, rz_sem,
):
    q = lax.axis_index("dom")
    e = lax.axis_index("elem")
    z, x = q // NX, q % NX

    def at_elem(by):
        return (q, (e + by) % N_ELEM)

    def at_dom(by):
        return ((q + by + N_DOM) % N_DOM, e)

    def at_x(by):
        return (z * NX + (x + by) % NX, e)

    def at_z(by):
        return (((z + by) % NZ) * NX + x, e)

    partners = (
        [at_elem(m) for m in range(1, N_ELEM)]
        + [at_dom(o) for o in OFFSETS]
        + [at_x(m) for m in range(1, NX)]
        + [at_z(m) for m in range(1, NZ)]
    )
    barrier = pltpu.get_barrier_semaphore()
    for partner in partners:
        pl.semaphore_signal(barrier, inc=1, device_id=partner, device_id_type=MESH)

    load_a = pltpu.make_async_copy(adj_in, A, load_sem.at[0])
    load_r = pltpu.make_async_copy(reg_in, R, load_sem.at[1])
    load_a.start()
    load_r.start()

    A2, S2 = A.reshape(1000, 128), S.reshape(1000, 128)
    for row in range(3):
        sendb[0, row, pl.ds(100, 4), :] = jnp.zeros((4, 128), F32)
        sendb[1, row, pl.ds(100, 4), :] = jnp.zeros((4, 128), F32)

    send_rows = [
        isend[...],
        jnp.concatenate([psend[0:1, :], psend[1:2, :]], axis=1),
        jnp.concatenate([psend[2:3, :], psend[3:4, :]], axis=1),
    ]

    def make_traces(s):
        lanes = [rows_of(row & 127, 8) for row in send_rows]
        faces = [rows_of(row >> 8, 8) for row in send_rows]
        halves = [rows_of((row >> 7) & 1, 4) == 1 for row in send_rows]

        def one_row(a, carry):
            for b in range(5):
                kept = [jnp.zeros((8, 128), F32)] * 3
                for f in range(6):
                    n0, na, nb = FACE_NODE[f]
                    v = A[n0 + na * a + nb * b]
                    for h in range(2):
                        pool[s, 2 * f + h, pl.ds(20 * a + 4 * b, 4), :] = v[4 * h : 4 * h + 4]
                    for t in range(3):
                        kept[t] = jnp.where(faces[t] == f, lane_take(v, lanes[t]), kept[t])
                for t in range(3):
                    sendb[s, t, pl.ds(20 * a + 4 * b, 4), :] = jnp.where(
                        halves[t], kept[t][4:8], kept[t][0:4]
                    )
            return carry

        lax.fori_loop(0, 5, one_row, 0)

    def start_sends(s):
        own = pltpu.make_async_copy(
            sendb.at[s, 0], pool.at[s, OWN + e, pl.ds(0, ROWS)], own_sem.at[s]
        )
        own.start()
        inner, outer = {}, []
        for m in ELEM_ORDER:
            inner[m] = pltpu.make_async_remote_copy(
                src_ref=sendb.at[s, 0],
                dst_ref=pool.at[s, OWN + e, pl.ds(0, ROWS)],
                send_sem=si_sem.at[s, m],
                recv_sem=ri_sem.at[s, m],
                device_id=at_elem(m),
                device_id_type=MESH,
            )
        for r, o in enumerate(OFFSETS):
            outer.append(
                pltpu.make_async_remote_copy(
                    src_ref=sendb.at[s, 1 + r // 2],
                    dst_ref=pool.at[s, FAR + r, pl.ds(0, ROWS)],
                    send_sem=sp_sem.at[s, r],
                    recv_sem=rp_sem.at[s, r],
                    device_id=at_dom(o),
                    device_id_type=MESH,
                )
            )
        for copy in [inner[4], outer[0], outer[3], inner[3], inner[5], outer[1], outer[2]]:
            copy.start()
        for m in (2, 6, 1, 7):
            inner[m].start()
        return own, inner, outer

    def component(s, chunk, c):
        return pool[s, chunk, pl.ds(c, 32, stride=4), :]

    link_all = link[...]
    near_link = jnp.where(link_all < 0, 0, link_all)
    far = near_link >= 2560
    lane_all = jnp.where(far, near_link - 2560, near_link) & 127
    chunk_all = jnp.where(far, FAR + ((near_link - 2560) >> 6), near_link >> 7)

    def face_row(table, f, h):
        return table[f : f + 1, 128 * h : 128 * h + 128]

    def gather_pass(s, chunks, first):
        for f in range(6):
            sign = -1.0 if f % 2 == 0 else 1.0
            kept, lane, chunk_of = [], [], []
            for h in range(2):
                kept.append(jnp.zeros((32, 128), F32) if first else G[2 * f + h])
                lane.append(rows_of(face_row(lane_all, f, h), 32))
                chunk_of.append(rows_of(face_row(chunk_all, f, h), 32))
            for chunk in chunks:
                values = component(s, chunk, 0) - sign * component(s, chunk, 1 + f // 2)
                for h in range(2):
                    kept[h] = jnp.where(chunk_of[h] == chunk, lane_take(values, lane[h]), kept[h])
            for h in range(2):
                G[2 * f + h] = kept[h]

    def volume(s):
        def comp(c):
            return jnp.concatenate(
                [A2[pl.ds(4 * h + c, 125, stride=8), :] for h in range(2)], axis=1
            )

        def precise(high_part, low_part, values):
            high, low = split(values)
            dot = functools.partial(jnp.dot, preferred_element_type=F32)
            return dot(high_part, high) + (dot(high_part, low) + dot(low_part, high))

        pressure = precise(dhigh[...], dlow[...], comp(0))
        total = None
        for d in range(3):
            scale = metric[d : d + 1, :]
            term = scale * precise(
                dhigh[pl.ds(128 * d, 128), :], dlow[pl.ds(128 * d, 128), :], comp(1 + d)
            )
            total = term if total is None else total + term
            grad = -scale * pressure[128 * d : 128 * d + 125]
            for h in range(2):
                S2[pl.ds(4 * h + 1 + d, 125, stride=8), :] = grad[:, 128 * h : 128 * h + 128]
        for h in range(2):
            S2[pl.ds(4 * h, 125, stride=8), :] = -total[0:125, 128 * h : 128 * h + 128]

    def add_rows(start, count, stride, values):
        where = pl.ds(start, count, stride=stride)
        S2[where, :] = S2[where, :] + values

    def fluxes(s):
        for f in range(6):
            d = f // 2
            sign = -1.0 if f % 2 == 0 else 1.0
            live_row = iota((32, 128), 0) < 25
            pair = jnp.concatenate(
                [jnp.where(live_row, G[2 * f + h], 0.0) for h in range(2)], axis=1
            )
            high, low = split(pair)
            variants = jnp.dot(
                perm[...], jnp.concatenate([high, low], axis=0), preferred_element_type=F32
            )
            for h in range(2):
                lanes = slice(128 * h, 128 * h + 128)
                turn = rows_of(face_row(orient, f, h), 32)
                near = variants[0:32, lanes]
                for symmetry in range(1, 8):
                    near = jnp.where(
                        turn == symmetry, variants[32 * symmetry : 32 * symmetry + 32, lanes], near
                    )
                p_own = component(s, 2 * f + h, 0)
                un_own = sign * component(s, 2 * f + h, 1 + d)
                wall_here = lane_take(wall[...], wslot[2 * f + h])
                is_wall = rows_of(face_row(link, f, h), 32) < 0
                near = jnp.where(is_wall, p_own + un_own - 2.0 * wall_here, near)
                lifted = (5.0 * metric[d : d + 1, lanes]) * (near - (p_own - un_own))
                n0, _, nb = FACE_NODE[f]
                for c, scale in ((0, 1.0), (1 + d, -sign)):
                    base = 8 * n0 + 4 * h + c
                    part = lifted if scale > 0 else -lifted
                    if d != 1:
                        add_rows(base, 25, 8 * nb, part[0:25])
                    else:
                        slot = 0 if scale > 0 else 1
                        lift[slot] = part
                        for a in range(5):
                            add_rows(base + 200 * a, 5, 8, lift[slot, pl.ds(5 * a, 5), :])

    def update(s):
        coef_a, coef_b = SECTION_A[s], SECTION_B[s]

        def step(i, carry):
            at = pl.ds(25 * i, 25)
            new = coef_a * R[at] + DT_STEP * S[at]
            R[at] = new
            A[at] = A[at] + coef_b * new
            return carry

        lax.fori_loop(0, 5, step, 0, unroll=True)

    patch = wpatch[...]
    live = wface[...] >= 0

    def patch_tables():
        lane8, chunk8 = rows_of(patch & 127, 8), rows_of(patch >> 7, 8)
        lane32 = rows_of(patch & 127, 32)
        counts = lane_take(pcount[...], lane32).astype(F32)
        mine = iota((32, 128), 0) == rows_of(patch >> 7, 32)
        count = jnp.sum(jnp.where(mine, counts, 0.0), axis=0, keepdims=True)
        active = (iota((8, 128), 0).astype(F32) < rows_of(count, 8)) & rows_of(live, 8)
        gain = jnp.zeros((8, 128), F32)
        rate = jnp.zeros((8, 128), F32)
        for c in range(32):
            lanes = pl.ds(128 * c, 128)
            ampb[pl.ds(0, 6), :] = amp[:, lanes]
            decb[pl.ds(0, 6), :] = decay[:, lanes]
            gain = jnp.where(chunk8 == c, lane_take(ampb[...], lane8), gain)
            rate = jnp.where(chunk8 == c, lane_take(decb[...], lane8), rate)
        six = iota((8, 128), 0) < 6
        active = active & six
        gain = jnp.where(active, gain, 0.0)
        rate = jnp.where(six, rate, 0.0)
        return jnp.where(active, 1.0, 0.0), gain, rate

    def slot_tables():
        face_column = jnp.transpose(rows_of(wface[...].astype(F32), 128))
        slot_column = iota((128, 128), 0).astype(F32)
        lane = iota((128, 128), 1).astype(F32)
        for j in range(12):
            hit = jnp.where(face_column == lane + 128.0 * j, slot_column, 0.0)
            wslot[j] = rows_of(jnp.sum(hit, axis=0, keepdims=True), 32).astype(I32)

    def walls(s, active, gain, rate):
        face_lane = rows_of(wface[...] & 127, 32)
        face_chunk = rows_of(wface[...] >> 7, 32)
        un = jnp.zeros((32, 128), F32)
        for f in range(6):
            sign = -1.0 if f % 2 == 0 else 1.0
            for h in range(2):
                taken = lane_take(component(s, 2 * f + h, 1 + f // 2), face_lane)
                un = jnp.where(face_chunk == 2 * f + h, sign * taken, un)
        uslot[...] = un
        un = uslot[pl.ds(0, 25), :]
        value = jnp.zeros((25, 128), F32)
        weighted = weights[...] * un
        aux_from, auxr_from = (aux_in, auxr_in) if s == 0 else (aux_out, auxr_out)
        for k in range(6):
            aux = aux_from[k]
            value = value + gain[k : k + 1] * aux
            fresh = jnp.sum(weighted * fwd[k, :, s, :].astype(F32), axis=0, keepdims=True)
            fresh = (SECTION_B[s] * DT_STEP) * active[k : k + 1] * fresh
            T[pl.ds(k, 1), :] = fresh if s == 0 else T[pl.ds(k, 1), :] + fresh
            rate_k = active[k : k + 1] * (un - rate[k : k + 1] * aux)
            new = SECTION_A[s] * auxr_from[k] + DT_STEP * rate_k
            auxr_out[k] = new
            aux_out[k] = aux + SECTION_B[s] * new
        wall[pl.ds(0, 25), :] = value

    def wait_halo(s, copies):
        own, inner, outer = copies
        own.wait()
        for m in ELEM_ORDER:
            inner[m].wait_recv()
        for copy in outer:
            copy.wait_recv()

    def wait_sent(copies):
        _, inner, outer = copies
        for m in ELEM_ORDER:
            inner[m].wait_send()
        for copy in outer:
            copy.wait_send()

    load_a.wait()
    make_traces(0)
    pl.semaphore_wait(barrier, len(partners))
    copies = start_sends(0)
    active, gain, rate = patch_tables()
    slot_tables()
    T[...] = jnp.zeros((8, 128), F32)
    T[pl.ds(6, 1), :] = patch.astype(F32)
    walls(0, active, gain, rate)
    volume(0)
    gather_pass(0, range(OWN), True)
    load_r.wait()
    wait_halo(0, copies)
    gather_pass(0, range(OWN, CHUNKS), False)
    fluxes(0)
    update(0)

    make_traces(1)
    copies_1 = start_sends(1)
    walls(1, active, gain, rate)
    Trecv[e] = T[...]
    sums = []
    for m in ELEM_ORDER:
        copy = pltpu.make_async_remote_copy(
            src_ref=T,
            dst_ref=Trecv.at[e],
            send_sem=sg_sem.at[m],
            recv_sem=rg_sem.at[m],
            device_id=at_elem(m),
            device_id_type=MESH,
        )
        copy.start()
        sums.append(copy)
    volume(1)
    gather_pass(1, range(OWN), True)

    for copy in sums:
        copy.wait_recv()
    column = iota((512, 128), 0).astype(F32)
    highs, lows = [], []
    for j in range(N_ELEM):
        ids = Trecv[j, pl.ds(6, 1), :].astype(I32)
        at = ((ids >> 6) & 3) * 128 + (ids >> 8) * 8 + (ids & 7)
        at = jnp.where(((ids >> 3) & 7) == e, at, -1).astype(F32)
        onehot[:, pl.ds(128 * j, 128)] = jnp.where(column == rows_of(at, 512), 1.0, 0.0).astype(
            jnp.bfloat16
        )
        high, low = split(Trecv[j])
        highs.append(high)
        lows.append(low)
    terms = jnp.concatenate(
        [jnp.concatenate(highs, axis=1), jnp.concatenate(lows, axis=1)], axis=0
    )
    binned = lax.dot_general(
        terms, onehot[...], (((1,), (1,)), ((), ())), preferred_element_type=F32
    )
    binned = binned[0:8] + binned[8:16]
    for j in range(NX):
        X[j] = binned[:, 128 * j : 128 * j + 128]
    Xrecv[x] = X[x]
    sums_x = []
    for m in range(1, NX):
        copy = pltpu.make_async_remote_copy(
            src_ref=X.at[(x + m) % NX],
            dst_ref=Xrecv.at[x],
            send_sem=sx_sem.at[m],
            recv_sem=rx_sem.at[m],
            device_id=at_x(m),
            device_id_type=MESH,
        )
        copy.start()
        sums_x.append(copy)

    wait_halo(1, copies_1)
    gather_pass(1, range(OWN, CHUNKS), False)

    for copy in sums_x:
        copy.wait_recv()
    summed = Xrecv[0] + Xrecv[1] + Xrecv[2] + Xrecv[3]
    lane16 = iota((8, 128), 1)
    for g in range(2):
        index = (8 * g + iota((8, 128), 0)) * 8 + (lane16 & 7)
        block = jnp.zeros((8, 128), F32)
        for k in range(6):
            block = jnp.where(
                (lane16 >> 3) == k, lane_take(rows_of(summed[k : k + 1], 8), index), block
            )
        for i in range(8):
            Z[8 * g + i] = block[i : i + 1]
    Zrecv[z] = Z[z]
    sums_z = []
    for m in range(1, NZ):
        copy = pltpu.make_async_remote_copy(
            src_ref=Z.at[(z + m) % NZ],
            dst_ref=Zrecv.at[z],
            send_sem=sz_sem.at[m],
            recv_sem=rz_sem.at[m],
            device_id=at_z(m),
            device_id_type=MESH,
        )
        copy.start()
        sums_z.append(copy)

    fluxes(1)
    update(1)
    store_a = pltpu.make_async_copy(A, adj_out, load_sem.at[0])
    store_r = pltpu.make_async_copy(R, reg_out, load_sem.at[1])
    store_a.start()
    store_r.start()

    for copy in sums_z:
        copy.wait_recv()
    row = Zrecv[0]
    for j in range(1, NZ):
        row = row + Zrecv[j]
    index = (iota((8, 128), 0) + 8 * iota((8, 128), 1)) & 127
    grad_out[...] = lane_take(rows_of(row, 8), index)[:, 0:6]

    wait_sent(copies)
    wait_sent(copies_1)
    for copy in sums + sums_x + sums_z:
        copy.wait_send()
    store_a.wait()
    store_r.wait()


def body(
    adjoint,
    adjoint_reg,
    metric,
    face_link,
    orient,
    intra_send,
    part_send,
    wall_face,
    wall_patch,
    pole_count,
    amplitude,
    pole_decay,
    wall_aux,
    wall_aux_reg,
    forward_aux,
):
    def packed(fields):
        return fields.reshape(4, 125, 2, 128).transpose(1, 2, 0, 3).reshape(125, 8, 128)

    def unpacked(nodes):
        return nodes.reshape(125, 2, 4, 128).transpose(2, 0, 1, 3).reshape(4, 125, 256)

    vmem = pl.BlockSpec(memory_space=pltpu.VMEM)
    hbm = pl.BlockSpec(memory_space=pl.ANY)
    dma = pltpu.SemaphoreType.DMA
    adj, reg, aux, auxr, grad = pl.pallas_call(
        kernel,
        out_shape=[
            jax.ShapeDtypeStruct((125, 8, 128), F32),
            jax.ShapeDtypeStruct((125, 8, 128), F32),
            jax.ShapeDtypeStruct((6, 25, 128), F32),
            jax.ShapeDtypeStruct((6, 25, 128), F32),
            jax.ShapeDtypeStruct((8, 6), F32),
        ],
        in_specs=[hbm, hbm] + [vmem] * 17,
        out_specs=[hbm, hbm] + [vmem] * 3,
        scratch_shapes=[
            pltpu.VMEM((125, 8, 128), F32),
            pltpu.VMEM((125, 8, 128), F32),
            pltpu.VMEM((125, 8, 128), F32),
            pltpu.VMEM((2, CHUNKS, 128, 128), F32),
            pltpu.VMEM((2, 3, ROWS, 128), F32),
            pltpu.VMEM((12, 32, 128), F32),
            pltpu.VMEM((2, 32, 128), F32),
            pltpu.VMEM((32, 128), F32),
            pltpu.VMEM((12, 32, 128), I32),
            pltpu.VMEM((32, 128), F32),
            pltpu.VMEM((8, 128), F32),
            pltpu.VMEM((8, 128), F32),
            pltpu.VMEM((8, 128), F32),
            pltpu.VMEM((N_ELEM, 8, 128), F32),
            pltpu.VMEM((512, 1024), jnp.bfloat16),
            pltpu.VMEM((NX, 8, 128), F32),
            pltpu.VMEM((NX, 8, 128), F32),
            pltpu.VMEM((NZ, 1, 128), F32),
            pltpu.VMEM((NZ, 1, 128), F32),
            dma((2,)),
            dma((2,)),
            dma((2, N_ELEM)),
            dma((2, N_ELEM)),
            dma((2, 4)),
            dma((2, 4)),
            dma((N_ELEM,)),
            dma((N_ELEM,)),
            dma((NX,)),
            dma((NX,)),
            dma((NZ,)),
            dma((NZ,)),
        ],
        compiler_params=pltpu.CompilerParams(
            collective_id=0, has_side_effects=True, vmem_limit_bytes=48 * 1024 * 1024
        ),
        cost_estimate=pl.CostEstimate(flops=400_000_000, bytes_accessed=3_000_000, transcendentals=0),
    )(
        packed(adjoint),
        packed(adjoint_reg),
        metric,
        face_link,
        orient,
        intra_send.reshape(1, 128),
        part_send,
        wall_face.reshape(1, 128),
        wall_patch.reshape(1, 128),
        pole_count.reshape(32, 128),
        amplitude.T,
        pole_decay.T,
        wall_aux,
        wall_aux_reg,
        forward_aux.transpose(1, 2, 0, 3),
        *constant_tables(),
    )
    return (unpacked(adj), unpacked(reg), aux, auxr, grad)


def solution(mesh):
    both = ("dom", "elem")
    in_specs = (
        P(None, None, both),
        P(None, None, both),
        P(None, both),
        P(None, both),
        P(None, both),
        P(both),
        P(None, both),
        P(both),
        P(both),
        P(),
        P(),
        P(),
        P(None, None, both),
        P(None, None, both),
        P(None, None, None, both),
    )
    out_specs = (
        P(None, None, both),
        P(None, None, both),
        P(None, None, both),
        P(None, None, both),
        P(both, None),
    )
    return jax.shard_map(body, mesh=mesh, in_specs=in_specs, out_specs=out_specs, check_vma=False)
```

```python
import functools

import jax
import jax.numpy as jnp
import numpy as np
from jax import lax
from jax.experimental import pallas as pl
from jax.experimental.pallas import tpu as pltpu
from jax.sharding import PartitionSpec as P

DT_STEP = 0.1
SECTION_A = (-1.514183444257, -1.697784692471)
SECTION_B = (0.1530572479681, 0.6994504559488)
OFFSETS = (-2, -1, 1, 2)
SAME_CORE = (4, 2, 6)
N_ELEM, N_DOM, NX, NZ = 8, 64, 4, 16
OWN, FAR = 12, 20
CHUNKS = 24
PLANE = tuple(
    sorted(
        ((dx, m) for dx in range(NX) for m in range(N_ELEM) if dx or m),
        key=lambda at: -min(at[0], NX - at[0]) - min(at[1], N_ELEM - at[1]) / 2,
    )
)
ROWS = 104
F32 = jnp.float32
I32 = jnp.int32
FACE_NODE = ((0, 5, 1), (100, 5, 1), (0, 25, 1), (20, 25, 1), (0, 25, 5), (4, 25, 5))
MESH = pl.DeviceIdType.MESH


def lobatto_tables():
    node_points = np.array([-1.0, -np.sqrt(3.0 / 7.0), 0.0, np.sqrt(3.0 / 7.0), 1.0])
    quad_line = np.array([0.1, 49.0 / 90.0, 32.0 / 45.0, 49.0 / 90.0, 0.1])
    bary_weight = np.array(
        [
            1.0 / np.prod([node_points[j] - node_points[k] for k in range(5) if k != j])
            for j in range(5)
        ]
    )
    line_deriv = np.zeros((5, 5))
    for i in range(5):
        for j in range(5):
            if i != j:
                line_deriv[i, j] = (
                    bary_weight[j] / bary_weight[i] / (node_points[i] - node_points[j])
                )
        line_deriv[i, i] = -np.sum(line_deriv[i])
    return (line_deriv, quad_line)


def constant_tables():
    line_deriv, quad_line = lobatto_tables()
    eye = np.eye(5)
    stack = np.zeros((3, 128, 125), np.float32)
    stack[0, :125] = np.kron(np.kron(line_deriv, eye), eye)
    stack[1, :125] = np.kron(np.kron(eye, line_deriv), eye)
    stack[2, :125] = np.kron(np.kron(eye, eye), line_deriv)
    stack = stack.reshape(384, 125)
    high = stack.astype(jnp.bfloat16)
    low = (stack - high.astype(np.float32)).astype(jnp.bfloat16)
    weights = np.broadcast_to(np.outer(quad_line, quad_line).reshape(25, 1), (25, 128))
    grid = np.arange(25).reshape(5, 5)
    perm = np.zeros((8, 32, 64), np.float32)
    for symmetry in range(8):
        variant = grid
        if symmetry & 4:
            variant = variant.T
        if symmetry & 1:
            variant = variant[::-1]
        if symmetry & 2:
            variant = variant[:, ::-1]
        for row, source in enumerate(variant.reshape(-1)):
            perm[symmetry, row, source] = 1.0
            perm[symmetry, row, 32 + source] = 1.0
    return (
        jnp.asarray(high),
        jnp.asarray(low),
        jnp.asarray(perm.reshape(256, 64), jnp.bfloat16),
        jnp.asarray(weights, F32),
    )


def lane_take(values, index):
    return jnp.take_along_axis(values, index, axis=1, mode="promise_in_bounds")


def split(values):
    high = values.astype(jnp.bfloat16)
    return high, (values - high.astype(F32)).astype(jnp.bfloat16)


def rows_of(row, count):
    return jnp.broadcast_to(row, (count, 128))


def iota(shape, dim):
    return lax.broadcasted_iota(I32, shape, dim)


def kernel(
    adj_hbm, reg_hbm, metric_hbm, link_hbm, orient_hbm, isend_hbm, psend_hbm, wface_hbm, wpatch_hbm,
    pcount_hbm, amp_hbm, decay_hbm, aux_hbm, auxr_hbm, fwd_hbm, dhigh_hbm, dlow_hbm, perm_hbm, weights_hbm,
    A, R, aux_out, auxr_out, grad_out,
    metric, link, orient, isend, psend, wface, wpatch, pcount, amp, decay, aux_in, auxr_in, fwd,
    dhigh, dlow, perm, weights, S, pool, sendb, outb, G, lift, wall, wslot, uslot, ampb, decb, T, Trecv, onehot, Z, Zrecv,
    load_sem, own_sem, si_sem, ri_sem, sr_sem, rr_sem, sp_sem, rp_sem, sg_sem, rg_sem, sz_sem, rz_sem,
):
    q = lax.axis_index("dom")
    e = lax.axis_index("elem")
    z, x = q // NX, q % NX

    def at_elem(by):
        return (q, (e + by) % N_ELEM)

    def at_dom(by):
        return ((q + by + N_DOM) % N_DOM, e)

    def at_xe(dx, m):
        return (z * NX + (x + dx) % NX, (e + m) % N_ELEM)

    def at_z(by):
        return (((z + by) % NZ) * NX + x, e)

    loads = {}
    for number, (name, source, target) in enumerate(
        (
            ("isend", isend_hbm, isend),
            ("psend", psend_hbm, psend),
            ("A", adj_hbm, A),
            ("wpatch", wpatch_hbm, wpatch),
            ("wface", wface_hbm, wface),
            ("link", link_hbm, link),
            ("metric", metric_hbm, metric),
            ("pcount", pcount_hbm, pcount),
            ("amp", amp_hbm, amp),
            ("decay", decay_hbm, decay),
            ("weights", weights_hbm, weights),
            ("aux", aux_hbm, aux_in),
            ("auxr", auxr_hbm, auxr_in),
            ("fwd", fwd_hbm, fwd),
            ("dhigh", dhigh_hbm, dhigh),
            ("dlow", dlow_hbm, dlow),
            ("orient", orient_hbm, orient),
            ("perm", perm_hbm, perm),
            ("R", reg_hbm, R),
        )
    ):
        loads[name] = pltpu.make_async_copy(source, target, load_sem.at[number])
    first = ("isend", "psend", "A")
    for name in first:
        loads[name].start()

    partners = (
        [at_xe(dx, m) for dx, m in PLANE]
        + [at_dom(o) for o in OFFSETS]
        + [at_z(m) for m in range(1, NZ)]
    )
    barrier = pltpu.get_barrier_semaphore()
    for partner in partners:
        pl.semaphore_signal(barrier, inc=1, device_id=partner, device_id_type=MESH)
    for name in loads:
        if name not in first:
            loads[name].start()

    def loaded(*names):
        for name in names:
            loads[name].wait()

    A2, S2 = A.reshape(1000, 128), S.reshape(1000, 128)
    for row in range(3):
        sendb[0, row, pl.ds(100, 4), :] = jnp.zeros((4, 128), F32)
        sendb[1, row, pl.ds(100, 4), :] = jnp.zeros((4, 128), F32)

    loaded("isend", "psend", "A")
    send_rows = [
        isend[...],
        jnp.concatenate([psend[0:1, :], psend[1:2, :]], axis=1),
        jnp.concatenate([psend[2:3, :], psend[3:4, :]], axis=1),
    ]

    def own_traces(s):
        def one_row(a, carry):
            for b in range(5):
                for f in range(6):
                    n0, na, nb = FACE_NODE[f]
                    v = A[n0 + na * a + nb * b]
                    for h in range(2):
                        pool[s, 2 * f + h, pl.ds(20 * a + 4 * b, 4), :] = v[4 * h : 4 * h + 4]
            return carry

        lax.fori_loop(0, 5, one_row, 0)

    def sent_traces(s):
        lanes = [rows_of(row & 127, 8) for row in send_rows]
        faces = [rows_of(row >> 8, 8) for row in send_rows]
        halves = [rows_of((row >> 7) & 1, 4) == 1 for row in send_rows]

        def one_row(a, carry):
            for b in range(5):
                kept = [jnp.zeros((8, 128), F32)] * 3
                for f in range(6):
                    n0, na, nb = FACE_NODE[f]
                    v = A[n0 + na * a + nb * b]
                    for t in range(3):
                        kept[t] = jnp.where(faces[t] == f, lane_take(v, lanes[t]), kept[t])
                for t in range(3):
                    sendb[s, t, pl.ds(20 * a + 4 * b, 4), :] = jnp.where(
                        halves[t], kept[t][4:8], kept[t][0:4]
                    )
            return carry

        lax.fori_loop(0, 5, one_row, 0)

    def pack_outer(s):
        left_short = iota((40, 128), 1) < 64
        for t in range(2):
            low, high = sendb[s, 1 + t, pl.ds(0, 64), :], sendb[s, 1 + t, pl.ds(64, 40), :]
            outb[s, 2 * t] = low
            outb[s, 2 * t, pl.ds(0, 40), :] = jnp.where(
                left_short, low[0:40], pltpu.roll(high, 64, 1)
            )
            turned = pltpu.roll(low, 64, 1)
            outb[s, 2 * t + 1] = turned
            outb[s, 2 * t + 1, pl.ds(0, 40), :] = jnp.where(left_short, turned[0:40], high)

    sibling = (q, e + 1 - 2 * (e % 2))

    def block_of(m):
        return OWN + (e + N_ELEM - m) % N_ELEM

    def inner_copies(s):
        return {
            m: pltpu.make_async_remote_copy(
                src_ref=sendb.at[s, 0],
                dst_ref=pool.at[s, OWN + e, pl.ds(0, ROWS)],
                send_sem=si_sem.at[s, m],
                recv_sem=ri_sem.at[s, m],
                device_id=at_elem(m) if m else sibling,
                device_id_type=MESH,
            )
            for m in (*SAME_CORE, 0)
        }

    def relay(s, m):
        copy = pltpu.make_async_remote_copy(
            src_ref=pool.at[s, block_of(m), pl.ds(0, ROWS)],
            dst_ref=pool.at[s, block_of(m), pl.ds(0, ROWS)],
            send_sem=sr_sem.at[s, m],
            recv_sem=rr_sem.at[s, m],
            device_id=sibling,
            device_id_type=MESH,
        )
        copy.start()
        return copy

    def relayed_block(m):
        return OWN + (e + 1 - 2 * (e % 2) + N_ELEM - m) % N_ELEM

    def start_halo(s):
        own, inner, outer = own_copy(s), inner_copies(s), outer_copies(s)
        inner[4].start()
        outer[0].start()
        outer[3].start()
        inner[2].start()
        inner[6].start()
        outer[1].start()
        outer[2].start()
        inner[0].start()
        own.start()
        return own, inner, outer

    def finish_halo(s, copies):
        own, inner, outer = copies
        relays = []
        for m in (2, 6):
            inner[m].wait_recv()
            relays.append(relay(s, m))
        own.wait()
        inner[0].wait_recv()
        other = OWN + e + 1 - 2 * (e % 2)
        gather_pass(s, [OWN + e, other, block_of(2), block_of(6)], False)
        inner[4].wait_recv()
        relays.append(relay(s, 4))
        for copy in outer:
            copy.wait_recv()
        gather_pass(s, [FAR, FAR + 1, FAR + 2, FAR + 3, block_of(4)], False)
        for copy in relays:
            copy.wait_recv()
        gather_pass(s, [relayed_block(m) for m in (2, 6, 4)], False)
        return [*inner.values(), *outer, *relays]

    def outer_copies(s):
        return [
            pltpu.make_async_remote_copy(
                src_ref=outb.at[s, r],
                dst_ref=pool.at[s, FAR + r, pl.ds(0, 64)],
                send_sem=sp_sem.at[s, r],
                recv_sem=rp_sem.at[s, r],
                device_id=at_dom(o),
                device_id_type=MESH,
            )
            for r, o in enumerate(OFFSETS)
        ]

    def own_copy(s):
        return pltpu.make_async_copy(
            sendb.at[s, 0], pool.at[s, OWN + e, pl.ds(0, ROWS)], own_sem.at[s]
        )

    def component(s, chunk, c):
        return pool[s, chunk, pl.ds(c, 32, stride=4), :]

    def face_row(table, f, h):
        return table[f : f + 1, 128 * h : 128 * h + 128]

    def gather_pass(s, chunks, first):
        for f in range(6):
            sign = -1.0 if f % 2 == 0 else 1.0
            kept, lane, chunk_of = [], [], []
            for h in range(2):
                kept.append(jnp.zeros((32, 128), F32) if first else G[2 * f + h])
                lane.append(rows_of(face_row(lane_all, f, h), 32))
                chunk_of.append(rows_of(face_row(chunk_all, f, h), 32))
            for chunk in chunks:
                if isinstance(chunk, int) and chunk >= FAR:
                    p, u = (
                        pool[s, chunk, pl.ds(c, 16, stride=4), :] for c in (0, 1 + f // 2)
                    )
                    values = p - sign * u
                    for h in range(2):
                        taken = jnp.concatenate(
                            [lane_take(values, lane[h][0:16]), lane_take(values, lane[h][16:32] + 64)],
                            axis=0,
                        )
                        kept[h] = jnp.where(chunk_of[h] == chunk, taken, kept[h])
                    continue
                values = component(s, chunk, 0) - sign * component(s, chunk, 1 + f // 2)
                for h in range(2):
                    kept[h] = jnp.where(chunk_of[h] == chunk, lane_take(values, lane[h]), kept[h])
            for h in range(2):
                G[2 * f + h] = kept[h]

    def volume(s):
        def comp(c):
            return jnp.concatenate(
                [A2[pl.ds(4 * h + c, 125, stride=8), :] for h in range(2)], axis=1
            )

        def precise(high_part, low_part, values):
            high, low = split(values)
            dot = functools.partial(jnp.dot, preferred_element_type=F32)
            return dot(high_part, high) + (dot(high_part, low) + dot(low_part, high))

        pressure = precise(dhigh[...], dlow[...], comp(0))
        total = None
        for d in range(3):
            scale = metric[d : d + 1, :]
            term = scale * precise(
                dhigh[pl.ds(128 * d, 128), :], dlow[pl.ds(128 * d, 128), :], comp(1 + d)
            )
            total = term if total is None else total + term
            grad = -scale * pressure[128 * d : 128 * d + 125]
            for h in range(2):
                S2[pl.ds(4 * h + 1 + d, 125, stride=8), :] = grad[:, 128 * h : 128 * h + 128]
        for h in range(2):
            S2[pl.ds(4 * h, 125, stride=8), :] = -total[0:125, 128 * h : 128 * h + 128]

    def add_rows(start, count, stride, values):
        where = pl.ds(start, count, stride=stride)
        S2[where, :] = S2[where, :] + values

    def fluxes(s):
        for f in range(6):
            d = f // 2
            sign = -1.0 if f % 2 == 0 else 1.0
            live_row = iota((32, 128), 0) < 25
            pair = jnp.concatenate(
                [jnp.where(live_row, G[2 * f + h], 0.0) for h in range(2)], axis=1
            )
            high, low = split(pair)
            variants = jnp.dot(
                perm[...], jnp.concatenate([high, low], axis=0), preferred_element_type=F32
            )
            for h in range(2):
                lanes = slice(128 * h, 128 * h + 128)
                turn = rows_of(face_row(orient, f, h), 32)
                near = variants[0:32, lanes]
                for symmetry in range(1, 8):
                    near = jnp.where(
                        turn == symmetry, variants[32 * symmetry : 32 * symmetry + 32, lanes], near
                    )
                p_own = component(s, 2 * f + h, 0)
                un_own = sign * component(s, 2 * f + h, 1 + d)
                wall_here = lane_take(wall[...], wslot[2 * f + h])
                is_wall = rows_of(face_row(link, f, h), 32) < 0
                near = jnp.where(is_wall, p_own + un_own - 2.0 * wall_here, near)
                lifted = (5.0 * metric[d : d + 1, lanes]) * (near - (p_own - un_own))
                n0, _, nb = FACE_NODE[f]
                for c, scale in ((0, 1.0), (1 + d, -sign)):
                    base = 8 * n0 + 4 * h + c
                    part = lifted if scale > 0 else -lifted
                    if d != 1:
                        add_rows(base, 25, 8 * nb, part[0:25])
                    else:
                        slot = 0 if scale > 0 else 1
                        lift[slot] = part
                        for a in range(5):
                            add_rows(base + 200 * a, 5, 8, lift[slot, pl.ds(5 * a, 5), :])

    def update(s):
        coef_a, coef_b = SECTION_A[s], SECTION_B[s]

        def step(i, carry):
            at = pl.ds(25 * i, 25)
            new = coef_a * R[at] + DT_STEP * S[at]
            R[at] = new
            A[at] = A[at] + coef_b * new
            return carry

        lax.fori_loop(0, 5, step, 0, unroll=True)

    def patch_tables():
        lane8, chunk8 = rows_of(patch & 127, 8), rows_of(patch >> 7, 8)
        lane32 = rows_of(patch & 127, 32)
        counts = lane_take(pcount[...], lane32).astype(F32)
        mine = iota((32, 128), 0) == rows_of(patch >> 7, 32)
        count = jnp.sum(jnp.where(mine, counts, 0.0), axis=0, keepdims=True)
        active = (iota((8, 128), 0).astype(F32) < rows_of(count, 8)) & rows_of(live, 8)
        gain = jnp.zeros((8, 128), F32)
        rate = jnp.zeros((8, 128), F32)
        for c in range(32):
            lanes = pl.ds(128 * c, 128)
            ampb[pl.ds(0, 6), :] = amp[:, lanes]
            decb[pl.ds(0, 6), :] = decay[:, lanes]
            gain = jnp.where(chunk8 == c, lane_take(ampb[...], lane8), gain)
            rate = jnp.where(chunk8 == c, lane_take(decb[...], lane8), rate)
        six = iota((8, 128), 0) < 6
        active = active & six
        gain = jnp.where(active, gain, 0.0)
        rate = jnp.where(six, rate, 0.0)
        return jnp.where(active, 1.0, 0.0), gain, rate

    def slot_tables():
        face_column = jnp.transpose(rows_of(wface[...].astype(F32), 128))
        slot_column = iota((128, 128), 0).astype(F32)
        lane = iota((128, 128), 1).astype(F32)
        for j in range(12):
            hit = jnp.where(face_column == lane + 128.0 * j, slot_column, 0.0)
            wslot[j] = rows_of(jnp.sum(hit, axis=0, keepdims=True), 32).astype(I32)

    def wall_terms(s, active):
        face_lane = rows_of(wface[...] & 127, 32)
        face_chunk = rows_of(wface[...] >> 7, 32)
        un = jnp.zeros((32, 128), F32)
        for f in range(6):
            sign = -1.0 if f % 2 == 0 else 1.0
            for h in range(2):
                taken = lane_take(component(s, 2 * f + h, 1 + f // 2), face_lane)
                un = jnp.where(face_chunk == 2 * f + h, sign * taken, un)
        uslot[...] = un
        weighted = weights[...] * uslot[pl.ds(0, 25), :]
        for k in range(6):
            fresh = jnp.sum(weighted * fwd[k, :, s, :].astype(F32), axis=0, keepdims=True)
            fresh = (SECTION_B[s] * DT_STEP) * active[k : k + 1] * fresh
            T[pl.ds(k, 1), :] = fresh if s == 0 else T[pl.ds(k, 1), :] + fresh

    def wall_update(s, active, gain, rate):
        un = uslot[pl.ds(0, 25), :]
        value = jnp.zeros((25, 128), F32)
        aux_from, auxr_from = (aux_in, auxr_in) if s == 0 else (aux_out, auxr_out)
        for k in range(6):
            aux = aux_from[k]
            value = value + gain[k : k + 1] * aux
            rate_k = active[k : k + 1] * (un - rate[k : k + 1] * aux)
            new = SECTION_A[s] * auxr_from[k] + DT_STEP * rate_k
            auxr_out[k] = new
            aux_out[k] = aux + SECTION_B[s] * new
        wall[pl.ds(0, 25), :] = value

    sent_traces(0)
    pack_outer(0)
    pl.semaphore_wait(barrier, len(partners))
    copies = start_halo(0)
    own_traces(0)
    loaded("wpatch", "wface", "link", "metric", "pcount", "amp", "decay")
    link_all = link[...]
    near_link = jnp.where(link_all < 0, 0, link_all)
    far = near_link >= 2560
    lane_all = jnp.where(far, (near_link - 2560) & 63, near_link & 127)
    chunk_all = jnp.where(far, FAR + ((near_link - 2560) >> 6), near_link >> 7)

    patch = wpatch[...]
    live = wface[...] >= 0
    active, gain, rate = patch_tables()
    slot_tables()
    loaded("weights", "aux", "auxr", "fwd", "dhigh", "dlow")
    T[...] = jnp.zeros((8, 128), F32)
    T[pl.ds(6, 1), :] = patch.astype(F32)
    wall_terms(0, active)
    wall_update(0, active, gain, rate)
    volume(0)
    gather_pass(0, range(OWN), True)
    loaded("orient", "perm", "R")
    sent = finish_halo(0, copies)
    fluxes(0)
    update(0)

    own_traces(1)
    wall_terms(1, active)
    sums = []
    for dx, m in PLANE:
        copy = pltpu.make_async_remote_copy(
            src_ref=T,
            dst_ref=Trecv.at[x * N_ELEM + e],
            send_sem=sg_sem.at[dx, m],
            recv_sem=rg_sem.at[dx, m],
            device_id=at_xe(dx, m),
            device_id_type=MESH,
        )
        copy.start()
        sums.append(copy)
    sent_traces(1)
    pack_outer(1)
    copies = start_halo(1)
    Trecv[x * N_ELEM + e] = T[...]
    wall_update(1, active, gain, rate)
    volume(1)
    gather_pass(1, range(OWN), True)

    for copy in sums:
        copy.wait_recv()
    column = iota((128, 128), 0)
    highs, lows = [], []
    for j in range(NX * N_ELEM):
        ids = Trecv[j, pl.ds(6, 1), :].astype(I32)
        at = (ids >> 8) * 8 + (ids & 7)
        at = jnp.where(((ids >> 3) & 31) == (q % NX) * N_ELEM + e, at, -1)
        onehot[:, pl.ds(128 * j, 128)] = jnp.where(column == rows_of(at, 128), 1.0, 0.0).astype(
            jnp.bfloat16
        )
        high, low = split(Trecv[j])
        highs.append(high)
        lows.append(low)
    terms = jnp.concatenate(
        [jnp.concatenate(highs, axis=1), jnp.concatenate(lows, axis=1)], axis=0
    )
    binned = lax.dot_general(
        terms, onehot[...], (((1,), (1,)), ((), ())), preferred_element_type=F32
    )
    summed = binned[0:8] + binned[8:16]
    lane16 = iota((8, 128), 1)
    for g in range(2):
        index = (8 * g + iota((8, 128), 0)) * 8 + (lane16 & 7)
        block = jnp.zeros((8, 128), F32)
        for k in range(6):
            block = jnp.where(
                (lane16 >> 3) == k, lane_take(rows_of(summed[k : k + 1], 8), index), block
            )
        for i in range(8):
            Z[8 * g + i] = block[i : i + 1]
    Zrecv[z] = Z[z]
    sums_z = []
    for m in range(1, NZ):
        copy = pltpu.make_async_remote_copy(
            src_ref=Z.at[(z + m) % NZ],
            dst_ref=Zrecv.at[z],
            send_sem=sz_sem.at[m],
            recv_sem=rz_sem.at[m],
            device_id=at_z(m),
            device_id_type=MESH,
        )
        copy.start()
        sums_z.append(copy)

    sent += finish_halo(1, copies)
    fluxes(1)
    update(1)

    for copy in sums_z:
        copy.wait_recv()
    row = Zrecv[0]
    for j in range(1, NZ):
        row = row + Zrecv[j]
    index = (iota((8, 128), 0) + 8 * iota((8, 128), 1)) & 127
    grad_out[...] = lane_take(rows_of(row, 8), index)[:, 0:6]

    for copy in sent + sums + sums_z:
        copy.wait_send()


def store_kernel(*refs):
    sources, targets, sem = refs[:5], refs[5:10], refs[10]
    copies = [
        pltpu.make_async_copy(source, target, sem.at[i])
        for i, (source, target) in enumerate(zip(sources, targets))
    ]
    for copy in copies:
        copy.start()
    for copy in copies:
        copy.wait()


def body(
    adjoint,
    adjoint_reg,
    metric,
    face_link,
    orient,
    intra_send,
    part_send,
    wall_face,
    wall_patch,
    pole_count,
    amplitude,
    pole_decay,
    wall_aux,
    wall_aux_reg,
    forward_aux,
):
    def packed(fields):
        return fields.reshape(4, 125, 2, 128).transpose(1, 2, 0, 3).reshape(125, 8, 128)

    def unpacked(nodes):
        return nodes.reshape(125, 2, 4, 128).transpose(2, 0, 1, 3).reshape(4, 125, 256)

    vmem = pl.BlockSpec(memory_space=pltpu.VMEM)
    hbm = pl.BlockSpec(memory_space=pltpu.HBM)
    dma = pltpu.SemaphoreType.DMA
    operands = [
        packed(adjoint),
        packed(adjoint_reg),
        metric,
        face_link,
        orient,
        intra_send.reshape(1, 128),
        part_send,
        wall_face.reshape(1, 128),
        wall_patch.reshape(1, 128),
        pole_count.reshape(32, 128),
        amplitude.T,
        pole_decay.T,
        wall_aux,
        wall_aux_reg,
        forward_aux.transpose(1, 2, 0, 3),
        *constant_tables(),
    ]
    outs = [
        jax.ShapeDtypeStruct((125, 8, 128), F32),
        jax.ShapeDtypeStruct((125, 8, 128), F32),
        jax.ShapeDtypeStruct((6, 25, 128), F32),
        jax.ShapeDtypeStruct((6, 25, 128), F32),
        jax.ShapeDtypeStruct((8, 6), F32),
    ]
    results = pl.pallas_call(
        kernel,
        out_shape=outs,
        in_specs=[hbm] * 19,
        out_specs=[vmem] * 5,
        scratch_shapes=[
            pltpu.VMEM((3, 256), F32),
            pltpu.VMEM((6, 256), I32),
            pltpu.VMEM((6, 256), I32),
            pltpu.VMEM((1, 128), I32),
            pltpu.VMEM((4, 64), I32),
            pltpu.VMEM((1, 128), I32),
            pltpu.VMEM((1, 128), I32),
            pltpu.VMEM((32, 128), I32),
            pltpu.VMEM((6, 4096), F32),
            pltpu.VMEM((6, 4096), F32),
            pltpu.VMEM((6, 25, 128), F32),
            pltpu.VMEM((6, 25, 128), F32),
            pltpu.VMEM((6, 25, 2, 128), jnp.bfloat16),
            pltpu.VMEM((384, 125), jnp.bfloat16),
            pltpu.VMEM((384, 125), jnp.bfloat16),
            pltpu.VMEM((256, 64), jnp.bfloat16),
            pltpu.VMEM((25, 128), F32),
            pltpu.VMEM((125, 8, 128), F32),
            pltpu.VMEM((2, CHUNKS, 128, 128), F32),
            pltpu.VMEM((2, 3, ROWS, 128), F32),
            pltpu.VMEM((2, 4, 64, 128), F32),
            pltpu.VMEM((12, 32, 128), F32),
            pltpu.VMEM((2, 32, 128), F32),
            pltpu.VMEM((32, 128), F32),
            pltpu.VMEM((12, 32, 128), I32),
            pltpu.VMEM((32, 128), F32),
            pltpu.VMEM((8, 128), F32),
            pltpu.VMEM((8, 128), F32),
            pltpu.VMEM((8, 128), F32),
            pltpu.VMEM((NX * N_ELEM, 8, 128), F32),
            pltpu.VMEM((128, 4096), jnp.bfloat16),
            pltpu.VMEM((NZ, 1, 128), F32),
            pltpu.VMEM((NZ, 1, 128), F32),
            dma((19,)),
            dma((2,)),
            dma((2, N_ELEM)),
            dma((2, N_ELEM)),
            dma((2, N_ELEM)),
            dma((2, N_ELEM)),
            dma((2, 4)),
            dma((2, 4)),
            dma((NX, N_ELEM)),
            dma((NX, N_ELEM)),
            dma((NZ,)),
            dma((NZ,)),
        ],
        compiler_params=pltpu.CompilerParams(
            collective_id=0, has_side_effects=True, vmem_limit_bytes=48 * 1024 * 1024
        ),
        cost_estimate=pl.CostEstimate(flops=400_000_000, bytes_accessed=3_000_000, transcendentals=0),
    )(
        *[pltpu.with_memory_space_constraint(value, pltpu.HBM) for value in operands]
    )
    adj, reg, aux, auxr, grad = pl.pallas_call(
        store_kernel,
        out_shape=outs,
        in_specs=[vmem] * 5,
        out_specs=[hbm] * 5,
        scratch_shapes=[dma((5,))],
    )(*[pltpu.with_memory_space_constraint(value, pltpu.VMEM) for value in results])
    return (unpacked(adj), unpacked(reg), aux, auxr, grad)


def solution(mesh):
    both = ("dom", "elem")
    in_specs = (
        P(None, None, both),
        P(None, None, both),
        P(None, both),
        P(None, both),
        P(None, both),
        P(both),
        P(None, both),
        P(both),
        P(both),
        P(),
        P(),
        P(),
        P(None, None, both),
        P(None, None, both),
        P(None, None, None, both),
    )
    out_specs = (
        P(None, None, both),
        P(None, None, both),
        P(None, None, both),
        P(None, None, both),
        P(both, None),
    )
    return jax.shard_map(body, mesh=mesh, in_specs=in_specs, out_specs=out_specs, check_vma=False)
```

```python
import functools

import jax
import jax.numpy as jnp
import numpy as np
from jax import lax
from jax.experimental import pallas as pl
from jax.experimental.pallas import tpu as pltpu
from jax.sharding import PartitionSpec as P

DT_STEP = 0.1
SECTION_A = (-1.514183444257, -1.697784692471)
SECTION_B = (0.1530572479681, 0.6994504559488)
OFFSETS = (-2, -1, 1, 2)
CROSS = (4,)
SAME_CORE = (4, 2, 6)
N_ELEM, N_DOM, NX, NZ = 8, 64, 4, 16
OWN, FAR = 12, 20
CHUNKS = 24
FARTHEST_Z = (8, 7, 9, 6, 10, 5, 11, 4, 12, 3, 13, 2, 14, 1, 15)
PLANE = tuple(
    sorted(
        ((dx, m) for dx in range(NX) for m in range(N_ELEM) if dx or m),
        key=lambda at: -min(at[0], NX - at[0]) - min(at[1], N_ELEM - at[1]) / 2,
    )
)
ROWS = 104
F32 = jnp.float32
I32 = jnp.int32
FACE_NODE = ((0, 5, 1), (100, 5, 1), (0, 25, 1), (20, 25, 1), (0, 25, 5), (4, 25, 5))
MESH = pl.DeviceIdType.MESH


def lobatto_tables():
    node_points = np.array([-1.0, -np.sqrt(3.0 / 7.0), 0.0, np.sqrt(3.0 / 7.0), 1.0])
    quad_line = np.array([0.1, 49.0 / 90.0, 32.0 / 45.0, 49.0 / 90.0, 0.1])
    bary_weight = np.array(
        [
            1.0 / np.prod([node_points[j] - node_points[k] for k in range(5) if k != j])
            for j in range(5)
        ]
    )
    line_deriv = np.zeros((5, 5))
    for i in range(5):
        for j in range(5):
            if i != j:
                line_deriv[i, j] = (
                    bary_weight[j] / bary_weight[i] / (node_points[i] - node_points[j])
                )
        line_deriv[i, i] = -np.sum(line_deriv[i])
    return (line_deriv, quad_line)


def constant_tables():
    line_deriv, quad_line = lobatto_tables()
    eye = np.eye(5)
    stack = np.zeros((3, 128, 125), np.float32)
    stack[0, :125] = np.kron(np.kron(line_deriv, eye), eye)
    stack[1, :125] = np.kron(np.kron(eye, line_deriv), eye)
    stack[2, :125] = np.kron(np.kron(eye, eye), line_deriv)
    stack = stack.reshape(384, 125)
    high = stack.astype(jnp.bfloat16)
    low = (stack - high.astype(np.float32)).astype(jnp.bfloat16)
    weights = np.broadcast_to(np.outer(quad_line, quad_line).reshape(25, 1), (25, 128))
    grid = np.arange(25).reshape(5, 5)
    perm = np.zeros((8, 32, 64), np.float32)
    for symmetry in range(8):
        variant = grid
        if symmetry & 4:
            variant = variant.T
        if symmetry & 1:
            variant = variant[::-1]
        if symmetry & 2:
            variant = variant[:, ::-1]
        for row, source in enumerate(variant.reshape(-1)):
            perm[symmetry, row, source] = 1.0
            perm[symmetry, row, 32 + source] = 1.0
    return (
        jnp.asarray(high),
        jnp.asarray(low),
        jnp.asarray(perm.reshape(256, 64), jnp.bfloat16),
        jnp.asarray(weights, F32),
    )


def lane_take(values, index):
    return jnp.take_along_axis(values, index, axis=1, mode="promise_in_bounds")


def split(values):
    high = values.astype(jnp.bfloat16)
    return high, (values - high.astype(F32)).astype(jnp.bfloat16)


def rows_of(row, count):
    return jnp.broadcast_to(row, (count, 128))


def iota(shape, dim):
    return lax.broadcasted_iota(I32, shape, dim)


def kernel(
    adj_hbm, reg_hbm, metric_hbm, link_hbm, orient_hbm, isend_hbm, psend_hbm, wface_hbm, wpatch_hbm,
    pcount_hbm, amp_hbm, decay_hbm, aux_hbm, auxr_hbm, fwd_hbm, dhigh_hbm, dlow_hbm, perm_hbm, weights_hbm,
    A, R, aux_out, auxr_out, grad_out,
    metric, link, orient, isend, psend, wface, wpatch, pcount, amp, decay, aux_in, auxr_in, fwd,
    dhigh, dlow, perm, weights, S, pool, sendb, outb, G, lift, wall, wslot, uslot, ampb, decb, T, Trecv, onehot, Z, Zrecv,
    load_sem, own_sem, si_sem, ri_sem, sc_sem, rc_sem, sr_sem, rr_sem, sp_sem, rp_sem, sg_sem, rg_sem, sz_sem, rz_sem,
):
    q = lax.axis_index("dom")
    e = lax.axis_index("elem")
    z, x = q // NX, q % NX

    def at_elem(by):
        return (q, (e + by) % N_ELEM)

    def at_dom(by):
        return ((q + by + N_DOM) % N_DOM, e)

    def at_xe(dx, m):
        return (z * NX + (x + dx) % NX, (e + m) % N_ELEM)

    def at_z(by):
        return (((z + by) % NZ) * NX + x, e)

    loads = {}
    for number, (name, source, target) in enumerate(
        (
            ("isend", isend_hbm, isend),
            ("psend", psend_hbm, psend),
            ("A", adj_hbm, A),
            ("wpatch", wpatch_hbm, wpatch),
            ("wface", wface_hbm, wface),
            ("link", link_hbm, link),
            ("metric", metric_hbm, metric),
            ("pcount", pcount_hbm, pcount),
            ("amp", amp_hbm, amp),
            ("decay", decay_hbm, decay),
            ("weights", weights_hbm, weights),
            ("aux", aux_hbm, aux_in),
            ("auxr", auxr_hbm, auxr_in),
            ("fwd", fwd_hbm, fwd),
            ("dhigh", dhigh_hbm, dhigh),
            ("dlow", dlow_hbm, dlow),
            ("orient", orient_hbm, orient),
            ("perm", perm_hbm, perm),
            ("R", reg_hbm, R),
        )
    ):
        loads[name] = pltpu.make_async_copy(source, target, load_sem.at[number])
    barrier = pltpu.get_barrier_semaphore()

    def greet(partners):
        for partner in partners:
            pl.semaphore_signal(barrier, inc=1, device_id=partner, device_id_type=MESH)

    greet([at_z(m) for m in FARTHEST_Z])
    first = ("isend", "psend", "A")
    for name in first:
        loads[name].start()
    greet([at_dom(o) for o in OFFSETS])
    greet([at_xe(dx, m) for dx, m in PLANE])
    greeted = NZ - 1 + len(OFFSETS) + len(PLANE)
    for name in loads:
        if name not in first:
            loads[name].start()

    def loaded(*names):
        for name in names:
            loads[name].wait()

    A2, S2 = A.reshape(1000, 128), S.reshape(1000, 128)
    for row in range(3):
        sendb[0, row, pl.ds(100, 4), :] = jnp.zeros((4, 128), F32)
        sendb[1, row, pl.ds(100, 4), :] = jnp.zeros((4, 128), F32)

    loaded("isend", "psend", "A")
    send_rows = [
        isend[...],
        jnp.concatenate([psend[0:1, :], psend[1:2, :]], axis=1),
        jnp.concatenate([psend[2:3, :], psend[3:4, :]], axis=1),
    ]

    def own_traces(s):
        def one_row(a, carry):
            for b in range(5):
                for f in range(6):
                    n0, na, nb = FACE_NODE[f]
                    v = A[n0 + na * a + nb * b]
                    for h in range(2):
                        pool[s, 2 * f + h, pl.ds(20 * a + 4 * b, 4), :] = v[4 * h : 4 * h + 4]
            return carry

        lax.fori_loop(0, 5, one_row, 0)

    def sent_traces(s, tables):
        lanes = [rows_of(row & 127, 8) for row in send_rows]
        faces = [rows_of(row >> 8, 8) for row in send_rows]
        halves = [rows_of((row >> 7) & 1, 4) == 1 for row in send_rows]

        def one_row(a, carry):
            for b in range(5):
                kept = {t: jnp.zeros((8, 128), F32) for t in tables}
                for f in range(6):
                    n0, na, nb = FACE_NODE[f]
                    v = A[n0 + na * a + nb * b]
                    for t in tables:
                        kept[t] = jnp.where(faces[t] == f, lane_take(v, lanes[t]), kept[t])
                for t in tables:
                    sendb[s, t, pl.ds(20 * a + 4 * b, 4), :] = jnp.where(
                        halves[t], kept[t][4:8], kept[t][0:4]
                    )
            return carry

        lax.fori_loop(0, 5, one_row, 0)

    def pack_outer(s):
        left_short = iota((40, 128), 1) < 64
        for t in range(2):
            low, high = sendb[s, 1 + t, pl.ds(0, 64), :], sendb[s, 1 + t, pl.ds(64, 40), :]
            outb[s, 2 * t] = low
            outb[s, 2 * t, pl.ds(0, 40), :] = jnp.where(
                left_short, low[0:40], pltpu.roll(high, 64, 1)
            )
            turned = pltpu.roll(low, 64, 1)
            outb[s, 2 * t + 1] = turned
            outb[s, 2 * t + 1, pl.ds(0, 40), :] = jnp.where(left_short, turned[0:40], high)

    sibling = (q, e + 1 - 2 * (e % 2))

    def block_of(m):
        return OWN + (e + N_ELEM - m) % N_ELEM

    def inner_copies(s):
        return {
            m: pltpu.make_async_remote_copy(
                src_ref=sendb.at[s, 0],
                dst_ref=pool.at[s, OWN + e, pl.ds(0, ROWS)],
                send_sem=si_sem.at[s, m],
                recv_sem=ri_sem.at[s, m],
                device_id=at_elem(m) if m else sibling,
                device_id_type=MESH,
            )
            for m in (*SAME_CORE, 0)
        }

    def cross_copies(s):
        return {
            m: pltpu.make_async_remote_copy(
                src_ref=sendb.at[s, 0],
                dst_ref=pool.at[s, OWN + e, pl.ds(0, ROWS)],
                send_sem=sc_sem.at[s, m],
                recv_sem=rc_sem.at[s, m],
                device_id=(q, (e + m + 1 - 2 * (e % 2)) % N_ELEM),
                device_id_type=MESH,
            )
            for m in CROSS
        }

    def relay(s, m):
        copy = pltpu.make_async_remote_copy(
            src_ref=pool.at[s, block_of(m), pl.ds(0, ROWS)],
            dst_ref=pool.at[s, block_of(m), pl.ds(0, ROWS)],
            send_sem=sr_sem.at[s, m],
            recv_sem=rr_sem.at[s, m],
            device_id=sibling,
            device_id_type=MESH,
        )
        copy.start()
        return copy

    def relayed_block(m):
        return OWN + (e + 1 - 2 * (e % 2) + N_ELEM - m) % N_ELEM

    def start_halo(s):
        own, inner, cross, outer = own_copy(s), inner_copies(s), cross_copies(s), outer_copies(s)
        sent_traces(s, (0,))
        if s == 0:
            pl.semaphore_wait(barrier, greeted)
        for copy in (inner[4], cross[4], inner[2], inner[6], inner[0], own):
            copy.start()
        sent_traces(s, (1, 2))
        pack_outer(s)
        for r in (0, 3, 1, 2):
            outer[r].start()
        return own, inner, cross, outer

    def finish_halo(s, copies):
        own, inner, cross, outer = copies
        relays = []

        def arrived(m):
            inner[m].wait_recv()
            if m not in cross:
                relays.append(relay(s, m))

        arrived(2)
        arrived(6)
        own.wait()
        inner[0].wait_recv()
        other = OWN + e + 1 - 2 * (e % 2)
        gather_pass(s, [OWN + e, other, block_of(2), block_of(6)], False)
        for copy in outer:
            copy.wait_recv()
        arrived(4)
        gather_pass(s, [FAR, FAR + 1, FAR + 2, FAR + 3, block_of(4)], False)
        for copy in [*cross.values(), *relays]:
            copy.wait_recv()
        gather_pass(s, [relayed_block(m) for m in (2, 6, 4)], False)
        return [*inner.values(), *cross.values(), *outer, *relays]

    def outer_copies(s):
        return [
            pltpu.make_async_remote_copy(
                src_ref=outb.at[s, r],
                dst_ref=pool.at[s, FAR + r, pl.ds(0, 64)],
                send_sem=sp_sem.at[s, r],
                recv_sem=rp_sem.at[s, r],
                device_id=at_dom(o),
                device_id_type=MESH,
            )
            for r, o in enumerate(OFFSETS)
        ]

    def own_copy(s):
        return pltpu.make_async_copy(
            sendb.at[s, 0], pool.at[s, OWN + e, pl.ds(0, ROWS)], own_sem.at[s]
        )

    def component(s, chunk, c):
        return pool[s, chunk, pl.ds(c, 32, stride=4), :]

    def face_row(table, f, h):
        return table[f : f + 1, 128 * h : 128 * h + 128]

    def gather_pass(s, chunks, first):
        for f in range(6):
            sign = -1.0 if f % 2 == 0 else 1.0
            kept, lane, chunk_of = [], [], []
            for h in range(2):
                kept.append(jnp.zeros((32, 128), F32) if first else G[2 * f + h])
                lane.append(rows_of(face_row(lane_all, f, h), 32))
                chunk_of.append(rows_of(face_row(chunk_all, f, h), 32))
            for chunk in chunks:
                if isinstance(chunk, int) and chunk >= FAR:
                    p, u = (
                        pool[s, chunk, pl.ds(c, 16, stride=4), :] for c in (0, 1 + f // 2)
                    )
                    values = p - sign * u
                    for h in range(2):
                        taken = jnp.concatenate(
                            [lane_take(values, lane[h][0:16]), lane_take(values, lane[h][16:32] + 64)],
                            axis=0,
                        )
                        kept[h] = jnp.where(chunk_of[h] == chunk, taken, kept[h])
                    continue
                values = component(s, chunk, 0) - sign * component(s, chunk, 1 + f // 2)
                for h in range(2):
                    kept[h] = jnp.where(chunk_of[h] == chunk, lane_take(values, lane[h]), kept[h])
            for h in range(2):
                G[2 * f + h] = kept[h]

    def volume(s):
        def comp(c):
            return jnp.concatenate(
                [A2[pl.ds(4 * h + c, 125, stride=8), :] for h in range(2)], axis=1
            )

        def precise(high_part, low_part, values):
            high, low = split(values)
            dot = functools.partial(jnp.dot, preferred_element_type=F32)
            return dot(high_part, high) + (dot(high_part, low) + dot(low_part, high))

        pressure = precise(dhigh[...], dlow[...], comp(0))
        total = None
        for d in range(3):
            scale = metric[d : d + 1, :]
            term = scale * precise(
                dhigh[pl.ds(128 * d, 128), :], dlow[pl.ds(128 * d, 128), :], comp(1 + d)
            )
            total = term if total is None else total + term
            grad = -scale * pressure[128 * d : 128 * d + 125]
            for h in range(2):
                S2[pl.ds(4 * h + 1 + d, 125, stride=8), :] = grad[:, 128 * h : 128 * h + 128]
        for h in range(2):
            S2[pl.ds(4 * h, 125, stride=8), :] = -total[0:125, 128 * h : 128 * h + 128]

    def add_rows(start, count, stride, values):
        where = pl.ds(start, count, stride=stride)
        S2[where, :] = S2[where, :] + values

    def fluxes(s):
        for f in range(6):
            d = f // 2
            sign = -1.0 if f % 2 == 0 else 1.0
            live_row = iota((32, 128), 0) < 25
            pair = jnp.concatenate(
                [jnp.where(live_row, G[2 * f + h], 0.0) for h in range(2)], axis=1
            )
            high, low = split(pair)
            variants = jnp.dot(
                perm[...], jnp.concatenate([high, low], axis=0), preferred_element_type=F32
            )
            for h in range(2):
                lanes = slice(128 * h, 128 * h + 128)
                turn = rows_of(face_row(orient, f, h), 32)
                near = variants[0:32, lanes]
                for symmetry in range(1, 8):
                    near = jnp.where(
                        turn == symmetry, variants[32 * symmetry : 32 * symmetry + 32, lanes], near
                    )
                p_own = component(s, 2 * f + h, 0)
                un_own = sign * component(s, 2 * f + h, 1 + d)
                wall_here = lane_take(wall[...], wslot[2 * f + h])
                is_wall = rows_of(face_row(link, f, h), 32) < 0
                near = jnp.where(is_wall, p_own + un_own - 2.0 * wall_here, near)
                lifted = (5.0 * metric[d : d + 1, lanes]) * (near - (p_own - un_own))
                n0, _, nb = FACE_NODE[f]
                for c, scale in ((0, 1.0), (1 + d, -sign)):
                    base = 8 * n0 + 4 * h + c
                    part = lifted if scale > 0 else -lifted
                    if d != 1:
                        add_rows(base, 25, 8 * nb, part[0:25])
                    else:
                        slot = 0 if scale > 0 else 1
                        lift[slot] = part
                        for a in range(5):
                            add_rows(base + 200 * a, 5, 8, lift[slot, pl.ds(5 * a, 5), :])

    def update(s):
        coef_a, coef_b = SECTION_A[s], SECTION_B[s]

        def step(i, carry):
            at = pl.ds(25 * i, 25)
            new = coef_a * R[at] + DT_STEP * S[at]
            R[at] = new
            A[at] = A[at] + coef_b * new
            return carry

        lax.fori_loop(0, 5, step, 0, unroll=True)

    def patch_tables():
        lane8, chunk8 = rows_of(patch & 127, 8), rows_of(patch >> 7, 8)
        lane32 = rows_of(patch & 127, 32)
        counts = lane_take(pcount[...], lane32).astype(F32)
        mine = iota((32, 128), 0) == rows_of(patch >> 7, 32)
        count = jnp.sum(jnp.where(mine, counts, 0.0), axis=0, keepdims=True)
        active = (iota((8, 128), 0).astype(F32) < rows_of(count, 8)) & rows_of(live, 8)
        gain = jnp.zeros((8, 128), F32)
        rate = jnp.zeros((8, 128), F32)
        for c in range(32):
            lanes = pl.ds(128 * c, 128)
            ampb[pl.ds(0, 6), :] = amp[:, lanes]
            decb[pl.ds(0, 6), :] = decay[:, lanes]
            gain = jnp.where(chunk8 == c, lane_take(ampb[...], lane8), gain)
            rate = jnp.where(chunk8 == c, lane_take(decb[...], lane8), rate)
        six = iota((8, 128), 0) < 6
        active = active & six
        gain = jnp.where(active, gain, 0.0)
        rate = jnp.where(six, rate, 0.0)
        return jnp.where(active, 1.0, 0.0), gain, rate

    def slot_tables():
        face_column = jnp.transpose(rows_of(wface[...].astype(F32), 128))
        slot_column = iota((128, 128), 0).astype(F32)
        lane = iota((128, 128), 1).astype(F32)
        for j in range(12):
            hit = jnp.where(face_column == lane + 128.0 * j, slot_column, 0.0)
            wslot[j] = rows_of(jnp.sum(hit, axis=0, keepdims=True), 32).astype(I32)

    def wall_terms(s, active):
        face_lane = rows_of(wface[...] & 127, 32)
        face_chunk = rows_of(wface[...] >> 7, 32)
        un = jnp.zeros((32, 128), F32)
        for f in range(6):
            sign = -1.0 if f % 2 == 0 else 1.0
            for h in range(2):
                taken = lane_take(component(s, 2 * f + h, 1 + f // 2), face_lane)
                un = jnp.where(face_chunk == 2 * f + h, sign * taken, un)
        uslot[...] = un
        weighted = weights[...] * uslot[pl.ds(0, 25), :]
        for k in range(6):
            fresh = jnp.sum(weighted * fwd[k, :, s, :].astype(F32), axis=0, keepdims=True)
            fresh = (SECTION_B[s] * DT_STEP) * active[k : k + 1] * fresh
            T[pl.ds(k, 1), :] = fresh if s == 0 else T[pl.ds(k, 1), :] + fresh

    def wall_update(s, active, gain, rate):
        un = uslot[pl.ds(0, 25), :]
        value = jnp.zeros((25, 128), F32)
        aux_from, auxr_from = (aux_in, auxr_in) if s == 0 else (aux_out, auxr_out)
        for k in range(6):
            aux = aux_from[k]
            value = value + gain[k : k + 1] * aux
            rate_k = active[k : k + 1] * (un - rate[k : k + 1] * aux)
            new = SECTION_A[s] * auxr_from[k] + DT_STEP * rate_k
            auxr_out[k] = new
            aux_out[k] = aux + SECTION_B[s] * new
        wall[pl.ds(0, 25), :] = value

    copies = start_halo(0)
    own_traces(0)
    loaded("wpatch", "wface", "link", "metric", "pcount", "amp", "decay")
    link_all = link[...]
    near_link = jnp.where(link_all < 0, 0, link_all)
    far = near_link >= 2560
    lane_all = jnp.where(far, (near_link - 2560) & 63, near_link & 127)
    chunk_all = jnp.where(far, FAR + ((near_link - 2560) >> 6), near_link >> 7)

    patch = wpatch[...]
    live = wface[...] >= 0
    active, gain, rate = patch_tables()
    slot_tables()
    loaded("weights", "aux", "auxr", "fwd", "dhigh", "dlow")
    T[...] = jnp.zeros((8, 128), F32)
    T[pl.ds(6, 1), :] = patch.astype(F32)
    wall_terms(0, active)
    wall_update(0, active, gain, rate)
    volume(0)
    gather_pass(0, range(OWN), True)
    loaded("orient", "perm", "R")
    sent = finish_halo(0, copies)
    fluxes(0)
    update(0)

    own_traces(1)
    wall_terms(1, active)
    slot = x * N_ELEM + e
    for dx, m in PLANE:
        pltpu.make_async_remote_copy(
            src_ref=T,
            dst_ref=Trecv.at[slot],
            send_sem=sg_sem,
            recv_sem=rg_sem,
            device_id=at_xe(dx, m),
            device_id_type=MESH,
        ).start()
    pltpu.make_async_copy(T, Trecv.at[slot], rg_sem).start()
    copies = start_halo(1)
    wall_update(1, active, gain, rate)
    volume(1)
    gather_pass(1, range(OWN), True)

    pltpu.make_async_copy(Trecv, Trecv, rg_sem).wait()
    column = iota((128, 128), 0)
    highs, lows = [], []
    for j in range(NX * N_ELEM):
        ids = Trecv[j, pl.ds(6, 1), :].astype(I32)
        at = (ids >> 8) * 8 + (ids & 7)
        at = jnp.where(((ids >> 3) & 31) == (q % NX) * N_ELEM + e, at, -1)
        onehot[:, pl.ds(128 * j, 128)] = jnp.where(column == rows_of(at, 128), 1.0, 0.0).astype(
            jnp.bfloat16
        )
        high, low = split(Trecv[j])
        highs.append(high)
        lows.append(low)
    terms = jnp.concatenate(
        [jnp.concatenate(highs, axis=1), jnp.concatenate(lows, axis=1)], axis=0
    )
    binned = lax.dot_general(
        terms, onehot[...], (((1,), (1,)), ((), ())), preferred_element_type=F32
    )
    summed = binned[0:8] + binned[8:16]
    lane16 = iota((8, 128), 1)
    for g in range(2):
        index = (8 * g + iota((8, 128), 0)) * 8 + (lane16 & 7)
        block = jnp.zeros((8, 128), F32)
        for k in range(6):
            block = jnp.where(
                (lane16 >> 3) == k, lane_take(rows_of(summed[k : k + 1], 8), index), block
            )
        for i in range(8):
            Z[8 * g + i] = block[i : i + 1]
    for m in FARTHEST_Z:
        pltpu.make_async_remote_copy(
            src_ref=Z.at[(z + m) % NZ],
            dst_ref=Zrecv.at[z],
            send_sem=sz_sem,
            recv_sem=rz_sem,
            device_id=at_z(m),
            device_id_type=MESH,
        ).start()
    pltpu.make_async_copy(Z.at[z], Zrecv.at[z], rz_sem).start()

    sent += finish_halo(1, copies)
    fluxes(1)
    update(1)

    for copy in sent:
        copy.wait_send()
    most = pl.ds(0, NX * N_ELEM - 1)
    pltpu.make_async_copy(Trecv.at[most], Trecv.at[most], sg_sem).wait()
    most = pl.ds(0, NZ - 1)
    pltpu.make_async_copy(Z.at[most], Z.at[most], sz_sem).wait()
    pltpu.make_async_copy(Zrecv, Zrecv, rz_sem).wait()
    row = Zrecv[0]
    for j in range(1, NZ):
        row = row + Zrecv[j]
    index = (iota((8, 128), 0) + 8 * iota((8, 128), 1)) & 127
    grad_out[...] = lane_take(rows_of(row, 8), index)[:, 0:6]


def store_kernel(*refs):
    sources, targets, sem = refs[:5], refs[5:10], refs[10]
    copies = [
        pltpu.make_async_copy(source, target, sem.at[i])
        for i, (source, target) in enumerate(zip(sources, targets))
    ]
    for copy in copies:
        copy.start()
    for copy in copies:
        copy.wait()


def body(
    adjoint,
    adjoint_reg,
    metric,
    face_link,
    orient,
    intra_send,
    part_send,
    wall_face,
    wall_patch,
    pole_count,
    amplitude,
    pole_decay,
    wall_aux,
    wall_aux_reg,
    forward_aux,
):
    def packed(fields):
        return fields.reshape(4, 125, 2, 128).transpose(1, 2, 0, 3).reshape(125, 8, 128)

    def unpacked(nodes):
        return nodes.reshape(125, 2, 4, 128).transpose(2, 0, 1, 3).reshape(4, 125, 256)

    vmem = pl.BlockSpec(memory_space=pltpu.VMEM)
    hbm = pl.BlockSpec(memory_space=pltpu.HBM)
    dma = pltpu.SemaphoreType.DMA
    operands = [
        packed(adjoint),
        packed(adjoint_reg),
        metric,
        face_link,
        orient,
        intra_send.reshape(1, 128),
        part_send,
        wall_face.reshape(1, 128),
        wall_patch.reshape(1, 128),
        pole_count.reshape(32, 128),
        amplitude.T,
        pole_decay.T,
        wall_aux,
        wall_aux_reg,
        forward_aux.transpose(1, 2, 0, 3),
        *constant_tables(),
    ]
    outs = [
        jax.ShapeDtypeStruct((125, 8, 128), F32),
        jax.ShapeDtypeStruct((125, 8, 128), F32),
        jax.ShapeDtypeStruct((6, 25, 128), F32),
        jax.ShapeDtypeStruct((6, 25, 128), F32),
        jax.ShapeDtypeStruct((8, 6), F32),
    ]
    results = pl.pallas_call(
        kernel,
        out_shape=outs,
        in_specs=[hbm] * 19,
        out_specs=[vmem] * 5,
        scratch_shapes=[
            pltpu.VMEM((3, 256), F32),
            pltpu.VMEM((6, 256), I32),
            pltpu.VMEM((6, 256), I32),
            pltpu.VMEM((1, 128), I32),
            pltpu.VMEM((4, 64), I32),
            pltpu.VMEM((1, 128), I32),
            pltpu.VMEM((1, 128), I32),
            pltpu.VMEM((32, 128), I32),
            pltpu.VMEM((6, 4096), F32),
            pltpu.VMEM((6, 4096), F32),
            pltpu.VMEM((6, 25, 128), F32),
            pltpu.VMEM((6, 25, 128), F32),
            pltpu.VMEM((6, 25, 2, 128), jnp.bfloat16),
            pltpu.VMEM((384, 125), jnp.bfloat16),
            pltpu.VMEM((384, 125), jnp.bfloat16),
            pltpu.VMEM((256, 64), jnp.bfloat16),
            pltpu.VMEM((25, 128), F32),
            pltpu.VMEM((125, 8, 128), F32),
            pltpu.VMEM((2, CHUNKS, 128, 128), F32),
            pltpu.VMEM((2, 3, ROWS, 128), F32),
            pltpu.VMEM((2, 4, 64, 128), F32),
            pltpu.VMEM((12, 32, 128), F32),
            pltpu.VMEM((2, 32, 128), F32),
            pltpu.VMEM((32, 128), F32),
            pltpu.VMEM((12, 32, 128), I32),
            pltpu.VMEM((32, 128), F32),
            pltpu.VMEM((8, 128), F32),
            pltpu.VMEM((8, 128), F32),
            pltpu.VMEM((8, 128), F32),
            pltpu.VMEM((NX * N_ELEM, 8, 128), F32),
            pltpu.VMEM((128, 4096), jnp.bfloat16),
            pltpu.VMEM((NZ, 1, 128), F32),
            pltpu.VMEM((NZ, 1, 128), F32),
            dma((19,)),
            dma((2,)),
            dma((2, N_ELEM)),
            dma((2, N_ELEM)),
            dma((2, N_ELEM)),
            dma((2, N_ELEM)),
            dma((2, N_ELEM)),
            dma((2, N_ELEM)),
            dma((2, 4)),
            dma((2, 4)),
            dma,
            dma,
            dma,
            dma,
        ],
        compiler_params=pltpu.CompilerParams(
            collective_id=0, has_side_effects=True, vmem_limit_bytes=48 * 1024 * 1024
        ),
        cost_estimate=pl.CostEstimate(flops=400_000_000, bytes_accessed=3_000_000, transcendentals=0),
    )(
        *[pltpu.with_memory_space_constraint(value, pltpu.HBM) for value in operands]
    )
    adj, reg, aux, auxr, grad = pl.pallas_call(
        store_kernel,
        out_shape=outs,
        in_specs=[vmem] * 5,
        out_specs=[hbm] * 5,
        scratch_shapes=[dma((5,))],
    )(*[pltpu.with_memory_space_constraint(value, pltpu.VMEM) for value in results])
    return (unpacked(adj), unpacked(reg), aux, auxr, grad)


def solution(mesh):
    both = ("dom", "elem")
    in_specs = (
        P(None, None, both),
        P(None, None, both),
        P(None, both),
        P(None, both),
        P(None, both),
        P(both),
        P(None, both),
        P(both),
        P(both),
        P(),
        P(),
        P(),
        P(None, None, both),
        P(None, None, both),
        P(None, None, None, both),
    )
    out_specs = (
        P(None, None, both),
        P(None, None, both),
        P(None, None, both),
        P(None, None, both),
        P(both, None),
    )
    return jax.shard_map(body, mesh=mesh, in_specs=in_specs, out_specs=out_specs, check_vma=False)
```

```python
import functools

import jax
import jax.numpy as jnp
import numpy as np
from jax import lax
from jax.experimental import pallas as pl
from jax.experimental.pallas import tpu as pltpu
from jax.sharding import PartitionSpec as P

DT_STEP = 0.1
SECTION_A = (-1.514183444257, -1.697784692471)
SECTION_B = (0.1530572479681, 0.6994504559488)
OFFSETS = (-2, -1, 1, 2)
CROSS = (4,)
SAME_CORE = (4, 2, 6)
N_ELEM, N_DOM, NX, NZ = 8, 64, 4, 16
OWN, FAR = 12, 20
CHUNKS = 24
FARTHEST_Z = (8, 7, 9, 6, 10, 5, 11, 4, 12, 3, 13, 2, 14, 1, 15)
PLANE = tuple(
    sorted(
        ((dx, m) for dx in range(NX) for m in range(N_ELEM) if dx or m),
        key=lambda at: -min(at[0], NX - at[0]) - min(at[1], N_ELEM - at[1]) / 2,
    )
)
ROWS = 104
F32 = jnp.float32
I32 = jnp.int32
FACE_NODE = ((0, 5, 1), (100, 5, 1), (0, 25, 1), (20, 25, 1), (0, 25, 5), (4, 25, 5))
MESH = pl.DeviceIdType.MESH


def lobatto_tables():
    node_points = np.array([-1.0, -np.sqrt(3.0 / 7.0), 0.0, np.sqrt(3.0 / 7.0), 1.0])
    quad_line = np.array([0.1, 49.0 / 90.0, 32.0 / 45.0, 49.0 / 90.0, 0.1])
    bary_weight = np.array(
        [
            1.0 / np.prod([node_points[j] - node_points[k] for k in range(5) if k != j])
            for j in range(5)
        ]
    )
    line_deriv = np.zeros((5, 5))
    for i in range(5):
        for j in range(5):
            if i != j:
                line_deriv[i, j] = (
                    bary_weight[j] / bary_weight[i] / (node_points[i] - node_points[j])
                )
        line_deriv[i, i] = -np.sum(line_deriv[i])
    return (line_deriv, quad_line)


def constant_tables():
    line_deriv, quad_line = lobatto_tables()
    eye = np.eye(5)
    stack = np.zeros((3, 128, 125), np.float32)
    stack[0, :125] = np.kron(np.kron(line_deriv, eye), eye)
    stack[1, :125] = np.kron(np.kron(eye, line_deriv), eye)
    stack[2, :125] = np.kron(np.kron(eye, eye), line_deriv)
    stack = stack.reshape(384, 125)
    high = stack.astype(jnp.bfloat16)
    low = (stack - high.astype(np.float32)).astype(jnp.bfloat16)
    weights = np.broadcast_to(np.outer(quad_line, quad_line).reshape(25, 1), (25, 128))
    grid = np.arange(25).reshape(5, 5)
    perm = np.zeros((8, 32, 64), np.float32)
    for symmetry in range(8):
        variant = grid
        if symmetry & 4:
            variant = variant.T
        if symmetry & 1:
            variant = variant[::-1]
        if symmetry & 2:
            variant = variant[:, ::-1]
        for row, source in enumerate(variant.reshape(-1)):
            perm[symmetry, row, source] = 1.0
            perm[symmetry, row, 32 + source] = 1.0
    return (
        jnp.asarray(high),
        jnp.asarray(low),
        jnp.asarray(perm.reshape(256, 64), jnp.bfloat16),
        jnp.asarray(weights, F32),
    )


def lane_take(values, index):
    return jnp.take_along_axis(values, index, axis=1, mode="promise_in_bounds")


def split(values):
    high = values.astype(jnp.bfloat16)
    return high, (values - high.astype(F32)).astype(jnp.bfloat16)


def rows_of(row, count):
    return jnp.broadcast_to(row, (count, 128))


def iota(shape, dim):
    return lax.broadcasted_iota(I32, shape, dim)


def kernel(
    adj_hbm, reg_hbm, metric_hbm, link_hbm, orient_hbm, isend_hbm, psend_hbm, wface_hbm, wpatch_hbm,
    pcount_hbm, amp_hbm, decay_hbm, aux_hbm, auxr_hbm, fwd_hbm, dhigh_hbm, dlow_hbm, perm_hbm, weights_hbm,
    A, R, aux_out, auxr_out, grad_out,
    metric, link, orient, isend, psend, wface, wpatch, pcount, amp, decay, aux_in, auxr_in, fwd,
    dhigh, dlow, perm, weights, S, pool, sendb, outb, G, lift, wall, wslot, uslot, ampb, decb, T, Trecv, onehot, Z, Zrecv,
    load_sem, own_sem, si_sem, ri_sem, sc_sem, rc_sem, sr_sem, rr_sem, sp_sem, rp_sem, sg_sem, rg_sem, sz_sem, rz_sem, known_sem,
):
    q = lax.axis_index("dom")
    e = lax.axis_index("elem")
    z, x = q // NX, q % NX

    def at_elem(by):
        return (q, (e + by) % N_ELEM)

    def at_dom(by):
        return ((q + by + N_DOM) % N_DOM, e)

    def at_xe(dx, m):
        return (z * NX + (x + dx) % NX, (e + m) % N_ELEM)

    def at_z(by):
        return (((z + by) % NZ) * NX + x, e)

    loads = {}
    for number, (name, source, target) in enumerate(
        (
            ("isend", isend_hbm, isend),
            ("psend", psend_hbm, psend),
            ("A", adj_hbm, A),
            ("wpatch", wpatch_hbm, wpatch),
            ("wface", wface_hbm, wface),
            ("link", link_hbm, link),
            ("metric", metric_hbm, metric),
            ("pcount", pcount_hbm, pcount),
            ("amp", amp_hbm, amp),
            ("decay", decay_hbm, decay),
            ("weights", weights_hbm, weights),
            ("aux", aux_hbm, aux_in),
            ("auxr", auxr_hbm, auxr_in),
            ("fwd", fwd_hbm, fwd),
            ("dhigh", dhigh_hbm, dhigh),
            ("dlow", dlow_hbm, dlow),
            ("orient", orient_hbm, orient),
            ("perm", perm_hbm, perm),
            ("R", reg_hbm, R),
        )
    ):
        loads[name] = pltpu.make_async_copy(source, target, load_sem.at[number])
    barrier = pltpu.get_barrier_semaphore()

    def greet(partners):
        for partner in partners:
            pl.semaphore_signal(barrier, inc=1, device_id=partner, device_id_type=MESH)

    first = ("isend", "psend", "A")
    for name in first:
        loads[name].start()
    greet([at_dom(o) for o in (-4, 4, -3, 3, -2, 2, -1, 1)])
    greet([at_elem(m) for m in range(1, N_ELEM)])
    greeted = 8 + N_ELEM - 1

    def vouch(step):
        for m in (2**step, NZ - 2**step):
            pl.semaphore_signal(known_sem.at[step], inc=1, device_id=at_z(m), device_id_type=MESH)

    def vouched(step):
        pl.semaphore_wait(known_sem.at[step], 2)

    for name in loads:
        if name not in first:
            loads[name].start()

    def loaded(*names):
        for name in names:
            loads[name].wait()

    A2, S2 = A.reshape(1000, 128), S.reshape(1000, 128)
    for row in range(3):
        sendb[0, row, pl.ds(100, 4), :] = jnp.zeros((4, 128), F32)
        sendb[1, row, pl.ds(100, 4), :] = jnp.zeros((4, 128), F32)

    loaded("isend", "psend", "A")
    send_rows = [
        isend[...],
        jnp.concatenate([psend[0:1, :], psend[1:2, :]], axis=1),
        jnp.concatenate([psend[2:3, :], psend[3:4, :]], axis=1),
    ]

    def own_traces(s):
        def one_row(a, carry):
            for b in range(5):
                for f in range(6):
                    n0, na, nb = FACE_NODE[f]
                    v = A[n0 + na * a + nb * b]
                    for h in range(2):
                        pool[s, 2 * f + h, pl.ds(20 * a + 4 * b, 4), :] = v[4 * h : 4 * h + 4]
            return carry

        lax.fori_loop(0, 5, one_row, 0)

    def sent_traces(s, tables):
        lanes = [rows_of(row & 127, 8) for row in send_rows]
        faces = [rows_of(row >> 8, 8) for row in send_rows]
        halves = [rows_of((row >> 7) & 1, 4) == 1 for row in send_rows]

        def one_row(a, carry):
            for b in range(5):
                kept = {t: jnp.zeros((8, 128), F32) for t in tables}
                for f in range(6):
                    n0, na, nb = FACE_NODE[f]
                    v = A[n0 + na * a + nb * b]
                    for t in tables:
                        kept[t] = jnp.where(faces[t] == f, lane_take(v, lanes[t]), kept[t])
                for t in tables:
                    sendb[s, t, pl.ds(20 * a + 4 * b, 4), :] = jnp.where(
                        halves[t], kept[t][4:8], kept[t][0:4]
                    )
            return carry

        lax.fori_loop(0, 5, one_row, 0)

    def pack_outer(s):
        left_short = iota((40, 128), 1) < 64
        for t in range(2):
            low, high = sendb[s, 1 + t, pl.ds(0, 64), :], sendb[s, 1 + t, pl.ds(64, 40), :]
            outb[s, 2 * t] = low
            outb[s, 2 * t, pl.ds(0, 40), :] = jnp.where(
                left_short, low[0:40], pltpu.roll(high, 64, 1)
            )
            turned = pltpu.roll(low, 64, 1)
            outb[s, 2 * t + 1] = turned
            outb[s, 2 * t + 1, pl.ds(0, 40), :] = jnp.where(left_short, turned[0:40], high)

    sibling = (q, e + 1 - 2 * (e % 2))

    def block_of(m):
        return OWN + (e + N_ELEM - m) % N_ELEM

    def inner_copies(s):
        return {
            m: pltpu.make_async_remote_copy(
                src_ref=sendb.at[s, 0],
                dst_ref=pool.at[s, OWN + e, pl.ds(0, ROWS)],
                send_sem=si_sem.at[s, m],
                recv_sem=ri_sem.at[s, m],
                device_id=at_elem(m) if m else sibling,
                device_id_type=MESH,
            )
            for m in (*SAME_CORE, 0)
        }

    def cross_copies(s):
        return {
            m: pltpu.make_async_remote_copy(
                src_ref=sendb.at[s, 0],
                dst_ref=pool.at[s, OWN + e, pl.ds(0, ROWS)],
                send_sem=sc_sem.at[s, m],
                recv_sem=rc_sem.at[s, m],
                device_id=(q, (e + m + 1 - 2 * (e % 2)) % N_ELEM),
                device_id_type=MESH,
            )
            for m in CROSS
        }

    def relay(s, m):
        copy = pltpu.make_async_remote_copy(
            src_ref=pool.at[s, block_of(m), pl.ds(0, ROWS)],
            dst_ref=pool.at[s, block_of(m), pl.ds(0, ROWS)],
            send_sem=sr_sem.at[s, m],
            recv_sem=rr_sem.at[s, m],
            device_id=sibling,
            device_id_type=MESH,
        )
        copy.start()
        return copy

    def relayed_block(m):
        return OWN + (e + 1 - 2 * (e % 2) + N_ELEM - m) % N_ELEM

    def start_halo(s):
        own, inner, cross, outer = own_copy(s), inner_copies(s), cross_copies(s), outer_copies(s)
        sent_traces(s, (0,))
        if s == 0:
            pl.semaphore_wait(barrier, greeted)
            vouch(0)
        for copy in (inner[4], cross[4], inner[2], inner[6], inner[0], own):
            copy.start()
        sent_traces(s, (1, 2))
        pack_outer(s)
        for r in (0, 3, 1, 2):
            outer[r].start()
        return own, inner, cross, outer

    def finish_halo(s, copies):
        own, inner, cross, outer = copies
        relays = []

        def arrived(m):
            inner[m].wait_recv()
            if m not in cross:
                relays.append(relay(s, m))

        arrived(2)
        arrived(6)
        own.wait()
        inner[0].wait_recv()
        other = OWN + e + 1 - 2 * (e % 2)
        gather_pass(s, [OWN + e, other, block_of(2), block_of(6)], False)
        for copy in outer:
            copy.wait_recv()
        arrived(4)
        gather_pass(s, [FAR, FAR + 1, FAR + 2, FAR + 3, block_of(4)], False)
        for copy in [*cross.values(), *relays]:
            copy.wait_recv()
        gather_pass(s, [relayed_block(m) for m in (2, 6, 4)], False)
        return [*inner.values(), *cross.values(), *outer, *relays]

    def outer_copies(s):
        return [
            pltpu.make_async_remote_copy(
                src_ref=outb.at[s, r],
                dst_ref=pool.at[s, FAR + r, pl.ds(0, 64)],
                send_sem=sp_sem.at[s, r],
                recv_sem=rp_sem.at[s, r],
                device_id=at_dom(o),
                device_id_type=MESH,
            )
            for r, o in enumerate(OFFSETS)
        ]

    def own_copy(s):
        return pltpu.make_async_copy(
            sendb.at[s, 0], pool.at[s, OWN + e, pl.ds(0, ROWS)], own_sem.at[s]
        )

    def component(s, chunk, c):
        return pool[s, chunk, pl.ds(c, 32, stride=4), :]

    def face_row(table, f, h):
        return table[f : f + 1, 128 * h : 128 * h + 128]

    def gather_pass(s, chunks, first):
        for f in range(6):
            sign = -1.0 if f % 2 == 0 else 1.0
            kept, lane, chunk_of = [], [], []
            for h in range(2):
                kept.append(jnp.zeros((32, 128), F32) if first else G[2 * f + h])
                lane.append(rows_of(face_row(lane_all, f, h), 32))
                chunk_of.append(rows_of(face_row(chunk_all, f, h), 32))
            for chunk in chunks:
                if isinstance(chunk, int) and chunk >= FAR:
                    p, u = (
                        pool[s, chunk, pl.ds(c, 16, stride=4), :] for c in (0, 1 + f // 2)
                    )
                    values = p - sign * u
                    for h in range(2):
                        taken = jnp.concatenate(
                            [lane_take(values, lane[h][0:16]), lane_take(values, lane[h][16:32] + 64)],
                            axis=0,
                        )
                        kept[h] = jnp.where(chunk_of[h] == chunk, taken, kept[h])
                    continue
                values = component(s, chunk, 0) - sign * component(s, chunk, 1 + f // 2)
                for h in range(2):
                    kept[h] = jnp.where(chunk_of[h] == chunk, lane_take(values, lane[h]), kept[h])
            for h in range(2):
                G[2 * f + h] = kept[h]

    def volume(s):
        def comp(c):
            return jnp.concatenate(
                [A2[pl.ds(4 * h + c, 125, stride=8), :] for h in range(2)], axis=1
            )

        def precise(high_part, low_part, values):
            high, low = split(values)
            dot = functools.partial(jnp.dot, preferred_element_type=F32)
            return dot(high_part, high) + (dot(high_part, low) + dot(low_part, high))

        pressure = precise(dhigh[...], dlow[...], comp(0))
        total = None
        for d in range(3):
            scale = metric[d : d + 1, :]
            term = scale * precise(
                dhigh[pl.ds(128 * d, 128), :], dlow[pl.ds(128 * d, 128), :], comp(1 + d)
            )
            total = term if total is None else total + term
            grad = -scale * pressure[128 * d : 128 * d + 125]
            for h in range(2):
                S2[pl.ds(4 * h + 1 + d, 125, stride=8), :] = grad[:, 128 * h : 128 * h + 128]
        for h in range(2):
            S2[pl.ds(4 * h, 125, stride=8), :] = -total[0:125, 128 * h : 128 * h + 128]

    def add_rows(start, count, stride, values):
        where = pl.ds(start, count, stride=stride)
        S2[where, :] = S2[where, :] + values

    def fluxes(s):
        for f in range(6):
            d = f // 2
            sign = -1.0 if f % 2 == 0 else 1.0
            live_row = iota((32, 128), 0) < 25
            pair = jnp.concatenate(
                [jnp.where(live_row, G[2 * f + h], 0.0) for h in range(2)], axis=1
            )
            high, low = split(pair)
            variants = jnp.dot(
                perm[...], jnp.concatenate([high, low], axis=0), preferred_element_type=F32
            )
            for h in range(2):
                lanes = slice(128 * h, 128 * h + 128)
                turn = rows_of(face_row(orient, f, h), 32)
                near = variants[0:32, lanes]
                for symmetry in range(1, 8):
                    near = jnp.where(
                        turn == symmetry, variants[32 * symmetry : 32 * symmetry + 32, lanes], near
                    )
                p_own = component(s, 2 * f + h, 0)
                un_own = sign * component(s, 2 * f + h, 1 + d)
                wall_here = lane_take(wall[...], wslot[2 * f + h])
                is_wall = rows_of(face_row(link, f, h), 32) < 0
                near = jnp.where(is_wall, p_own + un_own - 2.0 * wall_here, near)
                lifted = (5.0 * metric[d : d + 1, lanes]) * (near - (p_own - un_own))
                n0, _, nb = FACE_NODE[f]
                for c, scale in ((0, 1.0), (1 + d, -sign)):
                    base = 8 * n0 + 4 * h + c
                    part = lifted if scale > 0 else -lifted
                    if d != 1:
                        add_rows(base, 25, 8 * nb, part[0:25])
                    else:
                        slot = 0 if scale > 0 else 1
                        lift[slot] = part
                        for a in range(5):
                            add_rows(base + 200 * a, 5, 8, lift[slot, pl.ds(5 * a, 5), :])

    def update(s):
        coef_a, coef_b = SECTION_A[s], SECTION_B[s]

        def step(i, carry):
            at = pl.ds(25 * i, 25)
            new = coef_a * R[at] + DT_STEP * S[at]
            R[at] = new
            A[at] = A[at] + coef_b * new
            return carry

        lax.fori_loop(0, 5, step, 0, unroll=True)

    def patch_tables():
        lane8, chunk8 = rows_of(patch & 127, 8), rows_of(patch >> 7, 8)
        lane32 = rows_of(patch & 127, 32)
        counts = lane_take(pcount[...], lane32).astype(F32)
        mine = iota((32, 128), 0) == rows_of(patch >> 7, 32)
        count = jnp.sum(jnp.where(mine, counts, 0.0), axis=0, keepdims=True)
        active = (iota((8, 128), 0).astype(F32) < rows_of(count, 8)) & rows_of(live, 8)
        gain = jnp.zeros((8, 128), F32)
        rate = jnp.zeros((8, 128), F32)
        for c in range(32):
            lanes = pl.ds(128 * c, 128)
            ampb[pl.ds(0, 6), :] = amp[:, lanes]
            decb[pl.ds(0, 6), :] = decay[:, lanes]
            gain = jnp.where(chunk8 == c, lane_take(ampb[...], lane8), gain)
            rate = jnp.where(chunk8 == c, lane_take(decb[...], lane8), rate)
        six = iota((8, 128), 0) < 6
        active = active & six
        gain = jnp.where(active, gain, 0.0)
        rate = jnp.where(six, rate, 0.0)
        return jnp.where(active, 1.0, 0.0), gain, rate

    def slot_tables():
        face_column = jnp.transpose(rows_of(wface[...].astype(F32), 128))
        slot_column = iota((128, 128), 0).astype(F32)
        lane = iota((128, 128), 1).astype(F32)
        for j in range(12):
            hit = jnp.where(face_column == lane + 128.0 * j, slot_column, 0.0)
            wslot[j] = rows_of(jnp.sum(hit, axis=0, keepdims=True), 32).astype(I32)

    def wall_terms(s, active):
        face_lane = rows_of(wface[...] & 127, 32)
        face_chunk = rows_of(wface[...] >> 7, 32)
        un = jnp.zeros((32, 128), F32)
        for f in range(6):
            sign = -1.0 if f % 2 == 0 else 1.0
            for h in range(2):
                taken = lane_take(component(s, 2 * f + h, 1 + f // 2), face_lane)
                un = jnp.where(face_chunk == 2 * f + h, sign * taken, un)
        uslot[...] = un
        weighted = weights[...] * uslot[pl.ds(0, 25), :]
        for k in range(6):
            fresh = jnp.sum(weighted * fwd[k, :, s, :].astype(F32), axis=0, keepdims=True)
            fresh = (SECTION_B[s] * DT_STEP) * active[k : k + 1] * fresh
            T[pl.ds(k, 1), :] = fresh if s == 0 else T[pl.ds(k, 1), :] + fresh

    def wall_update(s, active, gain, rate):
        un = uslot[pl.ds(0, 25), :]
        value = jnp.zeros((25, 128), F32)
        aux_from, auxr_from = (aux_in, auxr_in) if s == 0 else (aux_out, auxr_out)
        for k in range(6):
            aux = aux_from[k]
            value = value + gain[k : k + 1] * aux
            rate_k = active[k : k + 1] * (un - rate[k : k + 1] * aux)
            new = SECTION_A[s] * auxr_from[k] + DT_STEP * rate_k
            auxr_out[k] = new
            aux_out[k] = aux + SECTION_B[s] * new
        wall[pl.ds(0, 25), :] = value

    copies = start_halo(0)
    own_traces(0)
    loaded("wpatch", "wface", "link", "metric", "pcount", "amp", "decay")
    link_all = link[...]
    near_link = jnp.where(link_all < 0, 0, link_all)
    far = near_link >= 2560
    lane_all = jnp.where(far, (near_link - 2560) & 63, near_link & 127)
    chunk_all = jnp.where(far, FAR + ((near_link - 2560) >> 6), near_link >> 7)

    patch = wpatch[...]
    live = wface[...] >= 0
    active, gain, rate = patch_tables()
    slot_tables()
    loaded("weights", "aux", "auxr", "fwd", "dhigh", "dlow")
    T[...] = jnp.zeros((8, 128), F32)
    T[pl.ds(6, 1), :] = patch.astype(F32)
    wall_terms(0, active)
    wall_update(0, active, gain, rate)
    volume(0)
    gather_pass(0, range(OWN), True)
    loaded("orient", "perm", "R")
    vouched(0)
    vouch(1)
    sent = finish_halo(0, copies)
    fluxes(0)
    update(0)

    own_traces(1)
    wall_terms(1, active)
    slot = x * N_ELEM + e
    for dx, m in PLANE:
        pltpu.make_async_remote_copy(
            src_ref=T,
            dst_ref=Trecv.at[slot],
            send_sem=sg_sem,
            recv_sem=rg_sem,
            device_id=at_xe(dx, m),
            device_id_type=MESH,
        ).start()
    pltpu.make_async_copy(T, Trecv.at[slot], rg_sem).start()
    vouched(1)
    vouch(2)
    copies = start_halo(1)
    wall_update(1, active, gain, rate)
    volume(1)
    gather_pass(1, range(OWN), True)

    pltpu.make_async_copy(Trecv, Trecv, rg_sem).wait()
    column = iota((128, 128), 0)
    highs, lows = [], []
    for j in range(NX * N_ELEM):
        ids = Trecv[j, pl.ds(6, 1), :].astype(I32)
        at = (ids >> 8) * 8 + (ids & 7)
        at = jnp.where(((ids >> 3) & 31) == (q % NX) * N_ELEM + e, at, -1)
        onehot[:, pl.ds(128 * j, 128)] = jnp.where(column == rows_of(at, 128), 1.0, 0.0).astype(
            jnp.bfloat16
        )
        high, low = split(Trecv[j])
        highs.append(high)
        lows.append(low)
    terms = jnp.concatenate(
        [jnp.concatenate(highs, axis=1), jnp.concatenate(lows, axis=1)], axis=0
    )
    binned = lax.dot_general(
        terms, onehot[...], (((1,), (1,)), ((), ())), preferred_element_type=F32
    )
    summed = binned[0:8] + binned[8:16]
    lane16 = iota((8, 128), 1)
    for g in range(2):
        index = (8 * g + iota((8, 128), 0)) * 8 + (lane16 & 7)
        block = jnp.zeros((8, 128), F32)
        for k in range(6):
            block = jnp.where(
                (lane16 >> 3) == k, lane_take(rows_of(summed[k : k + 1], 8), index), block
            )
        for i in range(8):
            Z[8 * g + i] = block[i : i + 1]
    vouched(2)
    for m in FARTHEST_Z:
        pltpu.make_async_remote_copy(
            src_ref=Z.at[(z + m) % NZ],
            dst_ref=Zrecv.at[z],
            send_sem=sz_sem,
            recv_sem=rz_sem,
            device_id=at_z(m),
            device_id_type=MESH,
        ).start()
    pltpu.make_async_copy(Z.at[z], Zrecv.at[z], rz_sem).start()

    sent += finish_halo(1, copies)
    fluxes(1)
    update(1)

    for copy in sent:
        copy.wait_send()
    most = pl.ds(0, NX * N_ELEM - 1)
    pltpu.make_async_copy(Trecv.at[most], Trecv.at[most], sg_sem).wait()
    most = pl.ds(0, NZ - 1)
    pltpu.make_async_copy(Z.at[most], Z.at[most], sz_sem).wait()
    pltpu.make_async_copy(Zrecv, Zrecv, rz_sem).wait()
    row = Zrecv[0]
    for j in range(1, NZ):
        row = row + Zrecv[j]
    index = (iota((8, 128), 0) + 8 * iota((8, 128), 1)) & 127
    grad_out[...] = lane_take(rows_of(row, 8), index)[:, 0:6]


def store_kernel(*refs):
    sources, targets, sem = refs[:5], refs[5:10], refs[10]
    copies = [
        pltpu.make_async_copy(source, target, sem.at[i])
        for i, (source, target) in enumerate(zip(sources, targets))
    ]
    for copy in copies:
        copy.start()
    for copy in copies:
        copy.wait()


def body(
    adjoint,
    adjoint_reg,
    metric,
    face_link,
    orient,
    intra_send,
    part_send,
    wall_face,
    wall_patch,
    pole_count,
    amplitude,
    pole_decay,
    wall_aux,
    wall_aux_reg,
    forward_aux,
):
    def packed(fields):
        return fields.reshape(4, 125, 2, 128).transpose(1, 2, 0, 3).reshape(125, 8, 128)

    def unpacked(nodes):
        return nodes.reshape(125, 2, 4, 128).transpose(2, 0, 1, 3).reshape(4, 125, 256)

    vmem = pl.BlockSpec(memory_space=pltpu.VMEM)
    hbm = pl.BlockSpec(memory_space=pltpu.HBM)
    dma = pltpu.SemaphoreType.DMA
    operands = [
        packed(adjoint),
        packed(adjoint_reg),
        metric,
        face_link,
        orient,
        intra_send.reshape(1, 128),
        part_send,
        wall_face.reshape(1, 128),
        wall_patch.reshape(1, 128),
        pole_count.reshape(32, 128),
        amplitude.T,
        pole_decay.T,
        wall_aux,
        wall_aux_reg,
        forward_aux.transpose(1, 2, 0, 3),
        *constant_tables(),
    ]
    outs = [
        jax.ShapeDtypeStruct((125, 8, 128), F32),
        jax.ShapeDtypeStruct((125, 8, 128), F32),
        jax.ShapeDtypeStruct((6, 25, 128), F32),
        jax.ShapeDtypeStruct((6, 25, 128), F32),
        jax.ShapeDtypeStruct((8, 6), F32),
    ]
    results = pl.pallas_call(
        kernel,
        out_shape=outs,
        in_specs=[hbm] * 19,
        out_specs=[vmem] * 5,
        scratch_shapes=[
            pltpu.VMEM((3, 256), F32),
            pltpu.VMEM((6, 256), I32),
            pltpu.VMEM((6, 256), I32),
            pltpu.VMEM((1, 128), I32),
            pltpu.VMEM((4, 64), I32),
            pltpu.VMEM((1, 128), I32),
            pltpu.VMEM((1, 128), I32),
            pltpu.VMEM((32, 128), I32),
            pltpu.VMEM((6, 4096), F32),
            pltpu.VMEM((6, 4096), F32),
            pltpu.VMEM((6, 25, 128), F32),
            pltpu.VMEM((6, 25, 128), F32),
            pltpu.VMEM((6, 25, 2, 128), jnp.bfloat16),
            pltpu.VMEM((384, 125), jnp.bfloat16),
            pltpu.VMEM((384, 125), jnp.bfloat16),
            pltpu.VMEM((256, 64), jnp.bfloat16),
            pltpu.VMEM((25, 128), F32),
            pltpu.VMEM((125, 8, 128), F32),
            pltpu.VMEM((2, CHUNKS, 128, 128), F32),
            pltpu.VMEM((2, 3, ROWS, 128), F32),
            pltpu.VMEM((2, 4, 64, 128), F32),
            pltpu.VMEM((12, 32, 128), F32),
            pltpu.VMEM((2, 32, 128), F32),
            pltpu.VMEM((32, 128), F32),
            pltpu.VMEM((12, 32, 128), I32),
            pltpu.VMEM((32, 128), F32),
            pltpu.VMEM((8, 128), F32),
            pltpu.VMEM((8, 128), F32),
            pltpu.VMEM((8, 128), F32),
            pltpu.VMEM((NX * N_ELEM, 8, 128), F32),
            pltpu.VMEM((128, 4096), jnp.bfloat16),
            pltpu.VMEM((NZ, 1, 128), F32),
            pltpu.VMEM((NZ, 1, 128), F32),
            dma((19,)),
            dma((2,)),
            dma((2, N_ELEM)),
            dma((2, N_ELEM)),
            dma((2, N_ELEM)),
            dma((2, N_ELEM)),
            dma((2, N_ELEM)),
            dma((2, N_ELEM)),
            dma((2, 4)),
            dma((2, 4)),
            dma,
            dma,
            dma,
            dma,
            pltpu.SemaphoreType.REGULAR((3,)),
        ],
        compiler_params=pltpu.CompilerParams(
            collective_id=0, has_side_effects=True, vmem_limit_bytes=48 * 1024 * 1024
        ),
        cost_estimate=pl.CostEstimate(flops=400_000_000, bytes_accessed=3_000_000, transcendentals=0),
    )(
        *[pltpu.with_memory_space_constraint(value, pltpu.HBM) for value in operands]
    )
    adj, reg, aux, auxr, grad = pl.pallas_call(
        store_kernel,
        out_shape=outs,
        in_specs=[vmem] * 5,
        out_specs=[hbm] * 5,
        scratch_shapes=[dma((5,))],
    )(*[pltpu.with_memory_space_constraint(value, pltpu.VMEM) for value in results])
    return (unpacked(adj), unpacked(reg), aux, auxr, grad)


def solution(mesh):
    both = ("dom", "elem")
    in_specs = (
        P(None, None, both),
        P(None, None, both),
        P(None, both),
        P(None, both),
        P(None, both),
        P(both),
        P(None, both),
        P(both),
        P(both),
        P(),
        P(),
        P(),
        P(None, None, both),
        P(None, None, both),
        P(None, None, None, both),
    )
    out_specs = (
        P(None, None, both),
        P(None, None, both),
        P(None, None, both),
        P(None, None, both),
        P(both, None),
    )
    return jax.shard_map(body, mesh=mesh, in_specs=in_specs, out_specs=out_specs, check_vma=False)
```

```python
import functools

import jax
import jax.numpy as jnp
import numpy as np
from jax import lax
from jax.experimental import pallas as pl
from jax.experimental.pallas import tpu as pltpu
from jax.sharding import PartitionSpec as P

DT_STEP = 0.1
SECTION_A = (-1.514183444257, -1.697784692471)
SECTION_B = (0.1530572479681, 0.6994504559488)
OFFSETS = (-2, -1, 1, 2)
CROSS = (4, 2, 6)
SAME_CORE = (4, 2, 6)
N_ELEM, N_DOM, NX, NZ = 8, 64, 4, 16
OWN, FAR = 12, 20
CHUNKS = 24
FARTHEST_Z = (8, 7, 9, 6, 10, 5, 11, 4, 12, 3, 13, 2, 14, 1, 15)
PLANE = tuple(
    sorted(
        ((dx, m) for dx in range(NX) for m in range(N_ELEM) if dx or m),
        key=lambda at: -min(at[0], NX - at[0]) - min(at[1], N_ELEM - at[1]) / 2,
    )
)
ROWS = 104
F32 = jnp.float32
I32 = jnp.int32
FACE_NODE = ((0, 5, 1), (100, 5, 1), (0, 25, 1), (20, 25, 1), (0, 25, 5), (4, 25, 5))
MESH = pl.DeviceIdType.MESH


def lobatto_tables():
    node_points = np.array([-1.0, -np.sqrt(3.0 / 7.0), 0.0, np.sqrt(3.0 / 7.0), 1.0])
    quad_line = np.array([0.1, 49.0 / 90.0, 32.0 / 45.0, 49.0 / 90.0, 0.1])
    bary_weight = np.array(
        [
            1.0 / np.prod([node_points[j] - node_points[k] for k in range(5) if k != j])
            for j in range(5)
        ]
    )
    line_deriv = np.zeros((5, 5))
    for i in range(5):
        for j in range(5):
            if i != j:
                line_deriv[i, j] = (
                    bary_weight[j] / bary_weight[i] / (node_points[i] - node_points[j])
                )
        line_deriv[i, i] = -np.sum(line_deriv[i])
    return (line_deriv, quad_line)


def constant_tables():
    line_deriv, quad_line = lobatto_tables()
    eye = np.eye(5)
    stack = np.zeros((3, 128, 125), np.float32)
    stack[0, :125] = np.kron(np.kron(line_deriv, eye), eye)
    stack[1, :125] = np.kron(np.kron(eye, line_deriv), eye)
    stack[2, :125] = np.kron(np.kron(eye, eye), line_deriv)
    stack = stack.reshape(384, 125)
    high = stack.astype(jnp.bfloat16)
    low = (stack - high.astype(np.float32)).astype(jnp.bfloat16)
    weights = np.broadcast_to(np.outer(quad_line, quad_line).reshape(25, 1), (25, 128))
    grid = np.arange(25).reshape(5, 5)
    perm = np.zeros((8, 32, 64), np.float32)
    for symmetry in range(8):
        variant = grid
        if symmetry & 4:
            variant = variant.T
        if symmetry & 1:
            variant = variant[::-1]
        if symmetry & 2:
            variant = variant[:, ::-1]
        for row, source in enumerate(variant.reshape(-1)):
            perm[symmetry, row, source] = 1.0
            perm[symmetry, row, 32 + source] = 1.0
    return (
        jnp.asarray(high),
        jnp.asarray(low),
        jnp.asarray(perm.reshape(256, 64), jnp.bfloat16),
        jnp.asarray(weights, F32),
    )


def lane_take(values, index):
    return jnp.take_along_axis(values, index, axis=1, mode="promise_in_bounds")


def split(values):
    high = values.astype(jnp.bfloat16)
    return high, (values - high.astype(F32)).astype(jnp.bfloat16)


def rows_of(row, count):
    return jnp.broadcast_to(row, (count, 128))


def iota(shape, dim):
    return lax.broadcasted_iota(I32, shape, dim)


def kernel(
    adj_hbm, reg_hbm, metric_hbm, link_hbm, orient_hbm, isend_hbm, psend_hbm, wface_hbm, wpatch_hbm,
    pcount_hbm, amp_hbm, decay_hbm, aux_hbm, auxr_hbm, fwd_hbm, dhigh_hbm, dlow_hbm, perm_hbm, weights_hbm,
    A, R, aux_out, auxr_out, grad_out,
    metric, link, orient, isend, psend, wface, wpatch, pcount, amp, decay, aux_in, auxr_in, fwd,
    dhigh, dlow, perm, weights, S, pool, sendb, outb, G, lift, wall, wslot, uslot, ampb, decb, T, Trecv, onehot, Z, Zrecv,
    load_sem, own_sem, si_sem, ri_sem, sc_sem, rc_sem, sr_sem, rr_sem, sp_sem, rp_sem, sg_sem, rg_sem, sz_sem, rz_sem, known_sem,
):
    q = lax.axis_index("dom")
    e = lax.axis_index("elem")
    z, x = q // NX, q % NX

    def at_elem(by):
        return (q, (e + by) % N_ELEM)

    def at_dom(by):
        return ((q + by + N_DOM) % N_DOM, e)

    def at_xe(dx, m):
        return (z * NX + (x + dx) % NX, (e + m) % N_ELEM)

    def at_z(by):
        return (((z + by) % NZ) * NX + x, e)

    loads = {}
    for number, (name, source, target) in enumerate(
        (
            ("isend", isend_hbm, isend),
            ("psend", psend_hbm, psend),
            ("A", adj_hbm, A),
            ("wpatch", wpatch_hbm, wpatch),
            ("wface", wface_hbm, wface),
            ("link", link_hbm, link),
            ("metric", metric_hbm, metric),
            ("pcount", pcount_hbm, pcount),
            ("amp", amp_hbm, amp),
            ("decay", decay_hbm, decay),
            ("weights", weights_hbm, weights),
            ("aux", aux_hbm, aux_in),
            ("auxr", auxr_hbm, auxr_in),
            ("fwd", fwd_hbm, fwd),
            ("dhigh", dhigh_hbm, dhigh),
            ("dlow", dlow_hbm, dlow),
            ("orient", orient_hbm, orient),
            ("perm", perm_hbm, perm),
            ("R", reg_hbm, R),
        )
    ):
        loads[name] = pltpu.make_async_copy(source, target, load_sem.at[number])
    barrier = pltpu.get_barrier_semaphore()

    def greet(partners):
        for partner in partners:
            pl.semaphore_signal(barrier, inc=1, device_id=partner, device_id_type=MESH)

    first = ("isend", "psend", "A")
    for name in first:
        loads[name].start()
    greet([at_dom(o) for o in (-4, 4, -3, 3, -2, 2, -1, 1)])
    greet([at_elem(m) for m in range(1, N_ELEM)])
    greeted = 8 + N_ELEM - 1

    def vouch(step):
        for m in (2**step, NZ - 2**step):
            pl.semaphore_signal(known_sem.at[step], inc=1, device_id=at_z(m), device_id_type=MESH)

    def vouched(step):
        pl.semaphore_wait(known_sem.at[step], 2)

    for name in loads:
        if name not in first:
            loads[name].start()

    def loaded(*names):
        for name in names:
            loads[name].wait()

    A2, S2 = A.reshape(1000, 128), S.reshape(1000, 128)
    for row in range(3):
        sendb[0, row, pl.ds(100, 4), :] = jnp.zeros((4, 128), F32)
        sendb[1, row, pl.ds(100, 4), :] = jnp.zeros((4, 128), F32)

    loaded("isend", "psend", "A")
    send_rows = [
        isend[...],
        jnp.concatenate([psend[0:1, :], psend[1:2, :]], axis=1),
        jnp.concatenate([psend[2:3, :], psend[3:4, :]], axis=1),
    ]

    def own_traces(s):
        def one_row(a, carry):
            for b in range(5):
                for f in range(6):
                    n0, na, nb = FACE_NODE[f]
                    v = A[n0 + na * a + nb * b]
                    for h in range(2):
                        pool[s, 2 * f + h, pl.ds(20 * a + 4 * b, 4), :] = v[4 * h : 4 * h + 4]
            return carry

        lax.fori_loop(0, 5, one_row, 0)

    def sent_traces(s, tables):
        lanes = [rows_of(row & 127, 8) for row in send_rows]
        faces = [rows_of(row >> 8, 8) for row in send_rows]
        halves = [rows_of((row >> 7) & 1, 4) == 1 for row in send_rows]

        def one_row(a, carry):
            for b in range(5):
                kept = {t: jnp.zeros((8, 128), F32) for t in tables}
                for f in range(6):
                    n0, na, nb = FACE_NODE[f]
                    v = A[n0 + na * a + nb * b]
                    for t in tables:
                        kept[t] = jnp.where(faces[t] == f, lane_take(v, lanes[t]), kept[t])
                for t in tables:
                    sendb[s, t, pl.ds(20 * a + 4 * b, 4), :] = jnp.where(
                        halves[t], kept[t][4:8], kept[t][0:4]
                    )
            return carry

        lax.fori_loop(0, 5, one_row, 0)

    def pack_outer(s):
        left_short = iota((40, 128), 1) < 64
        for t in range(2):
            low, high = sendb[s, 1 + t, pl.ds(0, 64), :], sendb[s, 1 + t, pl.ds(64, 40), :]
            outb[s, 2 * t] = low
            outb[s, 2 * t, pl.ds(0, 40), :] = jnp.where(
                left_short, low[0:40], pltpu.roll(high, 64, 1)
            )
            turned = pltpu.roll(low, 64, 1)
            outb[s, 2 * t + 1] = turned
            outb[s, 2 * t + 1, pl.ds(0, 40), :] = jnp.where(left_short, turned[0:40], high)

    sibling = (q, e + 1 - 2 * (e % 2))

    def block_of(m):
        return OWN + (e + N_ELEM - m) % N_ELEM

    def inner_copies(s):
        return {
            m: pltpu.make_async_remote_copy(
                src_ref=sendb.at[s, 0],
                dst_ref=pool.at[s, OWN + e, pl.ds(0, ROWS)],
                send_sem=si_sem.at[s, m],
                recv_sem=ri_sem.at[s, m],
                device_id=at_elem(m) if m else sibling,
                device_id_type=MESH,
            )
            for m in (*SAME_CORE, 0)
        }

    def cross_copies(s):
        return {
            m: pltpu.make_async_remote_copy(
                src_ref=sendb.at[s, 0],
                dst_ref=pool.at[s, OWN + e, pl.ds(0, ROWS)],
                send_sem=sc_sem.at[s, m],
                recv_sem=rc_sem.at[s, m],
                device_id=(q, (e + m + 1 - 2 * (e % 2)) % N_ELEM),
                device_id_type=MESH,
            )
            for m in CROSS
        }

    def relay(s, m):
        copy = pltpu.make_async_remote_copy(
            src_ref=pool.at[s, block_of(m), pl.ds(0, ROWS)],
            dst_ref=pool.at[s, block_of(m), pl.ds(0, ROWS)],
            send_sem=sr_sem.at[s, m],
            recv_sem=rr_sem.at[s, m],
            device_id=sibling,
            device_id_type=MESH,
        )
        copy.start()
        return copy

    def relayed_block(m):
        return OWN + (e + 1 - 2 * (e % 2) + N_ELEM - m) % N_ELEM

    def start_halo(s):
        own, inner, cross, outer = own_copy(s), inner_copies(s), cross_copies(s), outer_copies(s)
        sent_traces(s, (0,))
        if s == 0:
            pl.semaphore_wait(barrier, greeted)
            vouch(0)
        for copy in (inner[4], cross[4], inner[2], inner[6], cross[2], cross[6], inner[0], own):
            copy.start()
        sent_traces(s, (1, 2))
        pack_outer(s)
        for r in (0, 3, 1, 2):
            outer[r].start()
        return own, inner, cross, outer

    def finish_halo(s, copies):
        own, inner, cross, outer = copies
        relays = []

        def arrived(m):
            inner[m].wait_recv()
            if m not in cross:
                relays.append(relay(s, m))

        arrived(2)
        arrived(6)
        own.wait()
        inner[0].wait_recv()
        other = OWN + e + 1 - 2 * (e % 2)
        gather_pass(s, [OWN + e, other, block_of(2), block_of(6)], False)
        for copy in outer:
            copy.wait_recv()
        arrived(4)
        gather_pass(s, [FAR, FAR + 1, FAR + 2, FAR + 3, block_of(4)], False)
        for copy in [*cross.values(), *relays]:
            copy.wait_recv()
        gather_pass(s, [relayed_block(m) for m in (2, 6, 4)], False)
        return [*inner.values(), *cross.values(), *outer, *relays]

    def outer_copies(s):
        return [
            pltpu.make_async_remote_copy(
                src_ref=outb.at[s, r],
                dst_ref=pool.at[s, FAR + r, pl.ds(0, 64)],
                send_sem=sp_sem.at[s, r],
                recv_sem=rp_sem.at[s, r],
                device_id=at_dom(o),
                device_id_type=MESH,
            )
            for r, o in enumerate(OFFSETS)
        ]

    def own_copy(s):
        return pltpu.make_async_copy(
            sendb.at[s, 0], pool.at[s, OWN + e, pl.ds(0, ROWS)], own_sem.at[s]
        )

    def component(s, chunk, c):
        return pool[s, chunk, pl.ds(c, 32, stride=4), :]

    def face_row(table, f, h):
        return table[f : f + 1, 128 * h : 128 * h + 128]

    def gather_pass(s, chunks, first):
        for f in range(6):
            sign = -1.0 if f % 2 == 0 else 1.0
            kept, lane, chunk_of = [], [], []
            for h in range(2):
                kept.append(jnp.zeros((32, 128), F32) if first else G[2 * f + h])
                lane.append(rows_of(face_row(lane_all, f, h), 32))
                chunk_of.append(rows_of(face_row(chunk_all, f, h), 32))
            for chunk in chunks:
                if isinstance(chunk, int) and chunk >= FAR:
                    p, u = (
                        pool[s, chunk, pl.ds(c, 16, stride=4), :] for c in (0, 1 + f // 2)
                    )
                    values = p - sign * u
                    for h in range(2):
                        taken = jnp.concatenate(
                            [lane_take(values, lane[h][0:16]), lane_take(values, lane[h][16:32] + 64)],
                            axis=0,
                        )
                        kept[h] = jnp.where(chunk_of[h] == chunk, taken, kept[h])
                    continue
                values = component(s, chunk, 0) - sign * component(s, chunk, 1 + f // 2)
                for h in range(2):
                    kept[h] = jnp.where(chunk_of[h] == chunk, lane_take(values, lane[h]), kept[h])
            for h in range(2):
                G[2 * f + h] = kept[h]

    def volume(s):
        def comp(c):
            return jnp.concatenate(
                [A2[pl.ds(4 * h + c, 125, stride=8), :] for h in range(2)], axis=1
            )

        def precise(high_part, low_part, values):
            high, low = split(values)
            dot = functools.partial(jnp.dot, preferred_element_type=F32)
            return dot(high_part, high) + (dot(high_part, low) + dot(low_part, high))

        pressure = precise(dhigh[...], dlow[...], comp(0))
        total = None
        for d in range(3):
            scale = metric[d : d + 1, :]
            term = scale * precise(
                dhigh[pl.ds(128 * d, 128), :], dlow[pl.ds(128 * d, 128), :], comp(1 + d)
            )
            total = term if total is None else total + term
            grad = -scale * pressure[128 * d : 128 * d + 125]
            for h in range(2):
                S2[pl.ds(4 * h + 1 + d, 125, stride=8), :] = grad[:, 128 * h : 128 * h + 128]
        for h in range(2):
            S2[pl.ds(4 * h, 125, stride=8), :] = -total[0:125, 128 * h : 128 * h + 128]

    def add_rows(start, count, stride, values):
        where = pl.ds(start, count, stride=stride)
        S2[where, :] = S2[where, :] + values

    def fluxes(s):
        for f in range(6):
            d = f // 2
            sign = -1.0 if f % 2 == 0 else 1.0
            live_row = iota((32, 128), 0) < 25
            pair = jnp.concatenate(
                [jnp.where(live_row, G[2 * f + h], 0.0) for h in range(2)], axis=1
            )
            high, low = split(pair)
            variants = jnp.dot(
                perm[...], jnp.concatenate([high, low], axis=0), preferred_element_type=F32
            )
            for h in range(2):
                lanes = slice(128 * h, 128 * h + 128)
                turn = rows_of(face_row(orient, f, h), 32)
                near = variants[0:32, lanes]
                for symmetry in range(1, 8):
                    near = jnp.where(
                        turn == symmetry, variants[32 * symmetry : 32 * symmetry + 32, lanes], near
                    )
                p_own = component(s, 2 * f + h, 0)
                un_own = sign * component(s, 2 * f + h, 1 + d)
                wall_here = lane_take(wall[...], wslot[2 * f + h])
                is_wall = rows_of(face_row(link, f, h), 32) < 0
                near = jnp.where(is_wall, p_own + un_own - 2.0 * wall_here, near)
                lifted = (5.0 * metric[d : d + 1, lanes]) * (near - (p_own - un_own))
                n0, _, nb = FACE_NODE[f]
                for c, scale in ((0, 1.0), (1 + d, -sign)):
                    base = 8 * n0 + 4 * h + c
                    part = lifted if scale > 0 else -lifted
                    if d != 1:
                        add_rows(base, 25, 8 * nb, part[0:25])
                    else:
                        slot = 0 if scale > 0 else 1
                        lift[slot] = part
                        for a in range(5):
                            add_rows(base + 200 * a, 5, 8, lift[slot, pl.ds(5 * a, 5), :])

    def update(s):
        coef_a, coef_b = SECTION_A[s], SECTION_B[s]

        def step(i, carry):
            at = pl.ds(25 * i, 25)
            new = coef_a * R[at] + DT_STEP * S[at]
            R[at] = new
            A[at] = A[at] + coef_b * new
            return carry

        lax.fori_loop(0, 5, step, 0, unroll=True)

    def patch_tables():
        lane8, chunk8 = rows_of(patch & 127, 8), rows_of(patch >> 7, 8)
        lane32 = rows_of(patch & 127, 32)
        counts = lane_take(pcount[...], lane32).astype(F32)
        mine = iota((32, 128), 0) == rows_of(patch >> 7, 32)
        count = jnp.sum(jnp.where(mine, counts, 0.0), axis=0, keepdims=True)
        active = (iota((8, 128), 0).astype(F32) < rows_of(count, 8)) & rows_of(live, 8)
        gain = jnp.zeros((8, 128), F32)
        rate = jnp.zeros((8, 128), F32)
        for c in range(32):
            lanes = pl.ds(128 * c, 128)
            ampb[pl.ds(0, 6), :] = amp[:, lanes]
            decb[pl.ds(0, 6), :] = decay[:, lanes]
            gain = jnp.where(chunk8 == c, lane_take(ampb[...], lane8), gain)
            rate = jnp.where(chunk8 == c, lane_take(decb[...], lane8), rate)
        six = iota((8, 128), 0) < 6
        active = active & six
        gain = jnp.where(active, gain, 0.0)
        rate = jnp.where(six, rate, 0.0)
        return jnp.where(active, 1.0, 0.0), gain, rate

    def slot_tables():
        face_column = jnp.transpose(rows_of(wface[...].astype(F32), 128))
        slot_column = iota((128, 128), 0).astype(F32)
        lane = iota((128, 128), 1).astype(F32)
        for j in range(12):
            hit = jnp.where(face_column == lane + 128.0 * j, slot_column, 0.0)
            wslot[j] = rows_of(jnp.sum(hit, axis=0, keepdims=True), 32).astype(I32)

    def wall_terms(s, active):
        face_lane = rows_of(wface[...] & 127, 32)
        face_chunk = rows_of(wface[...] >> 7, 32)
        un = jnp.zeros((32, 128), F32)
        for f in range(6):
            sign = -1.0 if f % 2 == 0 else 1.0
            for h in range(2):
                n0, _, nb = FACE_NODE[f]
                base = 8 * n0 + 4 * h + 1 + f // 2
                if f // 2 != 1:
                    G[2 * f + h, pl.ds(0, 25), :] = A2[pl.ds(base, 25, stride=8 * nb), :]
                else:
                    for a in range(5):
                        G[2 * f + h, pl.ds(5 * a, 5), :] = A2[pl.ds(base + 200 * a, 5, stride=8), :]
                taken = lane_take(G[2 * f + h], face_lane)
                un = jnp.where(face_chunk == 2 * f + h, sign * taken, un)
        uslot[...] = un
        weighted = weights[...] * uslot[pl.ds(0, 25), :]
        for k in range(6):
            fresh = jnp.sum(weighted * fwd[k, :, s, :].astype(F32), axis=0, keepdims=True)
            fresh = (SECTION_B[s] * DT_STEP) * active[k : k + 1] * fresh
            T[pl.ds(k, 1), :] = fresh if s == 0 else T[pl.ds(k, 1), :] + fresh

    def wall_update(s, active, gain, rate):
        un = uslot[pl.ds(0, 25), :]
        value = jnp.zeros((25, 128), F32)
        aux_from, auxr_from = (aux_in, auxr_in) if s == 0 else (aux_out, auxr_out)
        for k in range(6):
            aux = aux_from[k]
            value = value + gain[k : k + 1] * aux
            rate_k = active[k : k + 1] * (un - rate[k : k + 1] * aux)
            new = SECTION_A[s] * auxr_from[k] + DT_STEP * rate_k
            auxr_out[k] = new
            aux_out[k] = aux + SECTION_B[s] * new
        wall[pl.ds(0, 25), :] = value

    copies = start_halo(0)
    own_traces(0)
    loaded("wpatch", "wface", "link", "metric", "pcount", "amp", "decay")
    link_all = link[...]
    near_link = jnp.where(link_all < 0, 0, link_all)
    far = near_link >= 2560
    lane_all = jnp.where(far, (near_link - 2560) & 63, near_link & 127)
    chunk_all = jnp.where(far, FAR + ((near_link - 2560) >> 6), near_link >> 7)

    patch = wpatch[...]
    live = wface[...] >= 0
    active, gain, rate = patch_tables()
    slot_tables()
    loaded("weights", "aux", "auxr", "fwd", "dhigh", "dlow")
    T[...] = jnp.zeros((8, 128), F32)
    T[pl.ds(6, 1), :] = patch.astype(F32)
    wall_terms(0, active)
    wall_update(0, active, gain, rate)
    volume(0)
    gather_pass(0, range(OWN), True)
    loaded("orient", "perm", "R")
    vouched(0)
    vouch(1)
    sent = finish_halo(0, copies)
    fluxes(0)
    update(0)

    wall_terms(1, active)
    slot = x * N_ELEM + e
    for dx, m in PLANE:
        pltpu.make_async_remote_copy(
            src_ref=T,
            dst_ref=Trecv.at[slot],
            send_sem=sg_sem,
            recv_sem=rg_sem,
            device_id=at_xe(dx, m),
            device_id_type=MESH,
        ).start()
    pltpu.make_async_copy(T, Trecv.at[slot], rg_sem).start()
    vouched(1)
    vouch(2)
    copies = start_halo(1)
    own_traces(1)
    wall_update(1, active, gain, rate)
    volume(1)
    gather_pass(1, range(OWN), True)

    pltpu.make_async_copy(Trecv, Trecv, rg_sem).wait()
    column = iota((128, 128), 0)
    highs, lows = [], []
    for j in range(NX * N_ELEM):
        ids = Trecv[j, pl.ds(6, 1), :].astype(I32)
        at = (ids >> 8) * 8 + (ids & 7)
        at = jnp.where(((ids >> 3) & 31) == (q % NX) * N_ELEM + e, at, -1)
        onehot[:, pl.ds(128 * j, 128)] = jnp.where(column == rows_of(at, 128), 1.0, 0.0).astype(
            jnp.bfloat16
        )
        high, low = split(Trecv[j])
        highs.append(high)
        lows.append(low)
    terms = jnp.concatenate(
        [jnp.concatenate(highs, axis=1), jnp.concatenate(lows, axis=1)], axis=0
    )
    binned = lax.dot_general(
        terms, onehot[...], (((1,), (1,)), ((), ())), preferred_element_type=F32
    )
    summed = binned[0:8] + binned[8:16]
    lane16 = iota((8, 128), 1)
    for g in range(2):
        index = (8 * g + iota((8, 128), 0)) * 8 + (lane16 & 7)
        block = jnp.zeros((8, 128), F32)
        for k in range(6):
            block = jnp.where(
                (lane16 >> 3) == k, lane_take(rows_of(summed[k : k + 1], 8), index), block
            )
        for i in range(8):
            Z[8 * g + i] = block[i : i + 1]
    vouched(2)
    for m in FARTHEST_Z:
        pltpu.make_async_remote_copy(
            src_ref=Z.at[(z + m) % NZ],
            dst_ref=Zrecv.at[z],
            send_sem=sz_sem,
            recv_sem=rz_sem,
            device_id=at_z(m),
            device_id_type=MESH,
        ).start()
    pltpu.make_async_copy(Z.at[z], Zrecv.at[z], rz_sem).start()

    sent += finish_halo(1, copies)
    fluxes(1)
    update(1)

    for copy in sent:
        copy.wait_send()
    most = pl.ds(0, NX * N_ELEM - 1)
    pltpu.make_async_copy(Trecv.at[most], Trecv.at[most], sg_sem).wait()
    most = pl.ds(0, NZ - 1)
    pltpu.make_async_copy(Z.at[most], Z.at[most], sz_sem).wait()
    pltpu.make_async_copy(Zrecv, Zrecv, rz_sem).wait()
    row = Zrecv[0]
    for j in range(1, NZ):
        row = row + Zrecv[j]
    index = (iota((8, 128), 0) + 8 * iota((8, 128), 1)) & 127
    grad_out[...] = lane_take(rows_of(row, 8), index)[:, 0:6]


def store_kernel(*refs):
    sources, targets, sem = refs[:5], refs[5:10], refs[10]
    copies = [
        pltpu.make_async_copy(source, target, sem.at[i])
        for i, (source, target) in enumerate(zip(sources, targets))
    ]
    for copy in copies:
        copy.start()
    for copy in copies:
        copy.wait()


def body(
    adjoint,
    adjoint_reg,
    metric,
    face_link,
    orient,
    intra_send,
    part_send,
    wall_face,
    wall_patch,
    pole_count,
    amplitude,
    pole_decay,
    wall_aux,
    wall_aux_reg,
    forward_aux,
):
    def packed(fields):
        return fields.reshape(4, 125, 2, 128).transpose(1, 2, 0, 3).reshape(125, 8, 128)

    def unpacked(nodes):
        return nodes.reshape(125, 2, 4, 128).transpose(2, 0, 1, 3).reshape(4, 125, 256)

    vmem = pl.BlockSpec(memory_space=pltpu.VMEM)
    hbm = pl.BlockSpec(memory_space=pltpu.HBM)
    dma = pltpu.SemaphoreType.DMA
    operands = [
        packed(adjoint),
        packed(adjoint_reg),
        metric,
        face_link,
        orient,
        intra_send.reshape(1, 128),
        part_send,
        wall_face.reshape(1, 128),
        wall_patch.reshape(1, 128),
        pole_count.reshape(32, 128),
        amplitude.T,
        pole_decay.T,
        wall_aux,
        wall_aux_reg,
        forward_aux.transpose(1, 2, 0, 3),
        *constant_tables(),
    ]
    outs = [
        jax.ShapeDtypeStruct((125, 8, 128), F32),
        jax.ShapeDtypeStruct((125, 8, 128), F32),
        jax.ShapeDtypeStruct((6, 25, 128), F32),
        jax.ShapeDtypeStruct((6, 25, 128), F32),
        jax.ShapeDtypeStruct((8, 6), F32),
    ]
    results = pl.pallas_call(
        kernel,
        out_shape=outs,
        in_specs=[hbm] * 19,
        out_specs=[vmem] * 5,
        scratch_shapes=[
            pltpu.VMEM((3, 256), F32),
            pltpu.VMEM((6, 256), I32),
            pltpu.VMEM((6, 256), I32),
            pltpu.VMEM((1, 128), I32),
            pltpu.VMEM((4, 64), I32),
            pltpu.VMEM((1, 128), I32),
            pltpu.VMEM((1, 128), I32),
            pltpu.VMEM((32, 128), I32),
            pltpu.VMEM((6, 4096), F32),
            pltpu.VMEM((6, 4096), F32),
            pltpu.VMEM((6, 25, 128), F32),
            pltpu.VMEM((6, 25, 128), F32),
            pltpu.VMEM((6, 25, 2, 128), jnp.bfloat16),
            pltpu.VMEM((384, 125), jnp.bfloat16),
            pltpu.VMEM((384, 125), jnp.bfloat16),
            pltpu.VMEM((256, 64), jnp.bfloat16),
            pltpu.VMEM((25, 128), F32),
            pltpu.VMEM((125, 8, 128), F32),
            pltpu.VMEM((2, CHUNKS, 128, 128), F32),
            pltpu.VMEM((2, 3, ROWS, 128), F32),
            pltpu.VMEM((2, 4, 64, 128), F32),
            pltpu.VMEM((12, 32, 128), F32),
            pltpu.VMEM((2, 32, 128), F32),
            pltpu.VMEM((32, 128), F32),
            pltpu.VMEM((12, 32, 128), I32),
            pltpu.VMEM((32, 128), F32),
            pltpu.VMEM((8, 128), F32),
            pltpu.VMEM((8, 128), F32),
            pltpu.VMEM((8, 128), F32),
            pltpu.VMEM((NX * N_ELEM, 8, 128), F32),
            pltpu.VMEM((128, 4096), jnp.bfloat16),
            pltpu.VMEM((NZ, 1, 128), F32),
            pltpu.VMEM((NZ, 1, 128), F32),
            dma((19,)),
            dma((2,)),
            dma((2, N_ELEM)),
            dma((2, N_ELEM)),
            dma((2, N_ELEM)),
            dma((2, N_ELEM)),
            dma((2, N_ELEM)),
            dma((2, N_ELEM)),
            dma((2, 4)),
            dma((2, 4)),
            dma,
            dma,
            dma,
            dma,
            pltpu.SemaphoreType.REGULAR((3,)),
        ],
        compiler_params=pltpu.CompilerParams(
            collective_id=0, has_side_effects=True, vmem_limit_bytes=48 * 1024 * 1024
        ),
        cost_estimate=pl.CostEstimate(flops=400_000_000, bytes_accessed=3_000_000, transcendentals=0),
    )(
        *[pltpu.with_memory_space_constraint(value, pltpu.HBM) for value in operands]
    )
    adj, reg, aux, auxr, grad = pl.pallas_call(
        store_kernel,
        out_shape=outs,
        in_specs=[vmem] * 5,
        out_specs=[hbm] * 5,
        scratch_shapes=[dma((5,))],
    )(*[pltpu.with_memory_space_constraint(value, pltpu.VMEM) for value in results])
    return (unpacked(adj), unpacked(reg), aux, auxr, grad)


def solution(mesh):
    both = ("dom", "elem")
    in_specs = (
        P(None, None, both),
        P(None, None, both),
        P(None, both),
        P(None, both),
        P(None, both),
        P(both),
        P(None, both),
        P(both),
        P(both),
        P(),
        P(),
        P(),
        P(None, None, both),
        P(None, None, both),
        P(None, None, None, both),
    )
    out_specs = (
        P(None, None, both),
        P(None, None, both),
        P(None, None, both),
        P(None, None, both),
        P(both, None),
    )
    return jax.shard_map(body, mesh=mesh, in_specs=in_specs, out_specs=out_specs, check_vma=False)
```
